32 devices in a mesh: orig: 8 (over y, x, core), dest: 4 (over z).
Axes of the slice: x: 2, y: 2, z: 4, core: 2. Of those that a mesh axis runs over, the one named last changes fastest.
Arguments:
- pair_field: bfloat16 [64, 64, 128], P('orig', 'dest'), may hold values from -6 to 6
- region_mask: int32 [64], replicated, may hold values 0 or 1
- region_count: int32 [1], replicated, may hold values from 1 to 64
- row_query: bfloat16 [1, 128, 128], replicated, may hold values from -17.5 to 17.5, as said below
- row_key: bfloat16 [1, 128, 128], replicated, may hold values from -0.36 to 0.36, as said below
- row_value: bfloat16 [1, 128, 128], replicated, may hold values from -0.5 to 0.5
- row_gate: bfloat16 [1, 128, 128], replicated, may hold values from -0.5 to 0.5
- row_gate_bias: float32 [1, 128], replicated, may hold values from -4 to 4
- row_out: bfloat16 [1, 128, 128], replicated, may hold values from -1.5 to 1.5
- col_query: bfloat16 [1, 128, 128], replicated, may hold values from -17.5 to 17.5, as said below
- col_key: bfloat16 [1, 128, 128], replicated, may hold values from -0.36 to 0.36, as said below
- col_value: bfloat16 [1, 128, 128], replicated, may hold values from -0.5 to 0.5
- col_gate: bfloat16 [1, 128, 128], replicated, may hold values from -0.5 to 0.5
- col_gate_bias: float32 [1, 128], replicated, may hold values from -4 to 4
- col_out: bfloat16 [1, 128, 128], replicated, may hold values from -1.5 to 1.5
Outputs:
- new_pair: bfloat16 [64, 64, 128], P('orig', 'dest')
The draws below stay inside these ranges and needn't reach their ends.
Inputs may be any that keep to these rules, and one draw needn't show every extreme that they name: `row_query`: row attention query weights. `row_key`: row attention key weights. `col_query`: column attention query weights. `col_key`: column attention key weights.
All inputs are finite; a program needn't handle non-finite values.
Results may differ from the reference program's by a relative error of at most 0.012.
Values may be sent and summed in bfloat16 or wider, within the bound.
No kernel may reach another device: no remote copies, remote signals or barrier semaphores. Data moves between devices by JAX's collectives and lax.ppermute only.
A program may use at most 64 MiB of HBM per device.

```python
import math
import jax
import jax.numpy as jnp
from jax import lax

C = 128
H = 4
LAYERS = 1
REGIONS = 64


def query_and_key(key, salt_value):
    base_key = jax.random.fold_in(key, salt_value)
    draw_one, draw_two = jax.random.split(base_key)
    key_weight = jnp.clip(jax.random.normal(draw_one, (LAYERS, C, C), jnp.float32), -4.0, 4.0) / math.sqrt(C)
    key_weight = jnp.clip(key_weight, -0.35, 0.35)
    noise_part = jnp.clip(jax.random.normal(draw_two, (LAYERS, C, C), jnp.float32), -4.0, 4.0) / math.sqrt(C)
    query_weight = 2.0 * noise_part
    query_weight = jnp.clip(query_weight, -17.5, 17.5)
    return (query_weight, key_weight)


def draw_row_query(key, part):
    return query_and_key(key, 101)[0].astype(jnp.bfloat16)


def draw_row_key(key, part):
    return query_and_key(key, 101)[1].astype(jnp.bfloat16)


def draw_col_query(key, part):
    return query_and_key(key, 203)[0].astype(jnp.bfloat16)


def draw_col_key(key, part):
    return query_and_key(key, 203)[1].astype(jnp.bfloat16)


def touch_ends(values, key, low, top_value):
    shape = values.shape
    spot = [jax.random.randint(jax.random.fold_in(key, axis), (), 0, shape[axis]) for axis in range(len(shape))]
    values = values.at[tuple(spot)].set(low)
    longest = shape.index(max(shape))
    spot[longest] = (spot[longest] + 1) % shape[longest]
    return values.at[tuple(spot)].set(top_value)


def levels(stream_key, extent, pieces, smallest, high):
    def one(axis_at, shards_of):
        draws = jax.random.uniform(jax.random.fold_in(jax.random.fold_in(stream_key, 6), axis_at), (shards_of,), jnp.float32, smallest / len(pieces), high / len(pieces))
        return jnp.repeat(jnp.exp(draws), extent[axis_at] // shards_of).reshape((-1,) + (1,) * (len(extent) - axis_at - 1))

    gain = one(*pieces[0])
    for cut in pieces[1:]:
        gain = gain * one(*cut)
    return gain


def centred(key, shape, width, most, pieces=(), kind=jnp.bfloat16):
    factor_of = levels(key, shape, pieces, -0.22, 0.18) if pieces else 1.0
    drawn = jax.random.normal(key, shape, jnp.float32) * width * factor_of
    return jnp.minimum(jnp.maximum(drawn, -most), most).astype(kind)


def setup_inputs(seed: int = 0) -> dict:
    splits = jax.random.split(jax.random.key(seed), 16)
    return {
        "pair_field": centred(splits[0], (REGIONS, REGIONS, C), 1.0, 6.0, ((0, 8), (1, 4))),
        "region_mask": touch_ends((jax.random.randint(splits[1], (REGIONS,), 0, 4) < 3).astype(jnp.int32), jax.random.fold_in(splits[1], 1), 0, 1),
        "region_count": jax.random.randint(splits[2], (1,), 1, REGIONS + 1).astype(jnp.int32),
        "row_query": draw_row_query(jax.random.fold_in(splits[15], 71), 0),
        "row_key": draw_row_key(jax.random.fold_in(splits[15], 71), 0),
        "row_value": centred(splits[5], (LAYERS, C, C), C ** -0.5, 0.5),
        "row_gate": centred(splits[6], (LAYERS, C, C), C ** -0.5, 0.5),
        "row_gate_bias": centred(splits[7], (LAYERS, C), 1.0, 4.0, (), jnp.float32),
        "row_out": centred(splits[8], (LAYERS, C, C), (C // 8) ** -0.5, 1.5),
        "col_query": draw_col_query(jax.random.fold_in(splits[15], 71), 0),
        "col_key": draw_col_key(jax.random.fold_in(splits[15], 71), 0),
        "col_value": centred(splits[11], (LAYERS, C, C), C ** -0.5, 0.5),
        "col_gate": centred(splits[12], (LAYERS, C, C), C ** -0.5, 0.5),
        "col_gate_bias": centred(splits[13], (LAYERS, C), 1.0, 4.0, (), jnp.float32),
        "col_out": centred(splits[14], (LAYERS, C, C), (C // 8) ** -0.5, 1.5),
    }


epsilon = 1e-05
masked_score = -1e+30

def normalize(pair_rows):
    widened = pair_rows.astype(jnp.float32)
    centered = widened - lax.optimization_barrier(jnp.mean(widened, axis=-1, keepdims=True))
    variance = lax.optimization_barrier(jnp.mean(centered * centered, axis=-1, keepdims=True))
    return (centered * lax.rsqrt(variance + epsilon)).astype(jnp.bfloat16)

def attend_rows(pair_rows, valid_keys, weights):
    w_query, w_key, w_value, w_gate, gate_bias, w_out = weights
    row_count, key_count, channels = pair_rows.shape
    head_size = channels // H
    normed = normalize(pair_rows)
    flattened = normed.reshape(row_count * key_count, channels)

    def project(weight):
        return jnp.dot(flattened, weight, preferred_element_type=jnp.float32)

    def heads_of(weight):
        return project(weight).astype(jnp.bfloat16).reshape(row_count // 8, 8, key_count, H, head_size)
    queries = heads_of(w_query)
    key_rows = heads_of(w_key)
    value_rows = heads_of(w_value)
    gate_values = jax.nn.sigmoid(project(w_gate) + gate_bias[None, :])

    def one_block(operands):
        block_queries, block_keys, block_values = operands
        scores = jnp.einsum('bqhd,bkhd->bhqk', block_queries.astype(jnp.float32), block_keys.astype(jnp.float32), precision=lax.Precision.HIGHEST) / math.sqrt(head_size)
        scores = jnp.where(valid_keys[None, None, None, :], scores, masked_score)
        maximum = lax.optimization_barrier(jnp.max(scores, axis=3, keepdims=True))
        expanded = jnp.exp(scores - maximum)
        block_weights = (expanded / lax.optimization_barrier(jnp.sum(expanded, axis=3, keepdims=True))).astype(jnp.bfloat16)
        return jnp.einsum('bhqk,bkhd->bqhd', block_weights.astype(jnp.float32), block_values.astype(jnp.float32), precision=lax.Precision.HIGHEST).astype(jnp.bfloat16)
    attended = lax.map(one_block, (queries, key_rows, value_rows)).reshape(row_count * key_count, channels)
    gated = (gate_values * attended.astype(jnp.float32)).astype(jnp.bfloat16)
    update = jnp.dot(gated, w_out, preferred_element_type=jnp.float32).reshape(row_count, key_count, channels)
    return (pair_rows.astype(jnp.float32) + update).astype(jnp.bfloat16)

def reference(pair_field, region_mask, region_count, row_query, row_key, row_value, row_gate, row_gate_bias, row_out, col_query, col_key, col_value, col_gate, col_gate_bias, col_out):
    positions = jnp.arange(REGIONS, dtype=jnp.int32)
    valid_keys = ((region_mask == 1) | (positions == 0)) & (positions < region_count[0])
    current = pair_field
    for layer_index in range(LAYERS):
        row_weights = (row_query[layer_index], row_key[layer_index], row_value[layer_index], row_gate[layer_index], row_gate_bias[layer_index], row_out[layer_index])
        col_weights = (col_query[layer_index], col_key[layer_index], col_value[layer_index], col_gate[layer_index], col_gate_bias[layer_index], col_out[layer_index])
        current = attend_rows(current, valid_keys, row_weights)
        turned = jnp.transpose(current, (1, 0, 2))
        current = jnp.transpose(attend_rows(turned, valid_keys, col_weights), (1, 0, 2))
    return current
```

```python
import functools
import math

import jax
import jax.numpy as jnp
from jax import lax
from jax.experimental import pallas as pl
from jax.experimental.pallas import tpu as pltpu
from jax.sharding import PartitionSpec as P

H = 4

epsilon = 1e-05
masked_score = -1e30
lanes = 128
group_rows = 1024

vmem = pl.BlockSpec(memory_space=pltpu.VMEM)


def packing(items, length):
    pack = max(p for p in range(1, items + 1) if items % p == 0 and (p == 1 or p * length <= lanes))
    group = max(
        g
        for g in range(pack, items + 1, pack)
        if items % g == 0 and (g == pack or g * length <= group_rows)
    )
    return pack, group


def prepare_kernel(axes, steps, parts, packs, mask_ref, count_ref, *refs):
    weights, gate_biases, outs, sem = refs[:10], refs[10:12], refs[12:18], refs[18]
    channels = weights[0].shape[1]
    copies = []
    for a in range(2):
        for w in range(5):
            copies.append(
                pltpu.make_async_copy(
                    weights[5 * a + w].at[0],
                    outs[3 * a].at[:, pl.ds(w * channels, channels)],
                    sem.at[len(copies)],
                )
            )
        copies.append(pltpu.make_async_copy(gate_biases[a], outs[3 * a + 1], sem.at[len(copies)]))
    for copy in copies:
        copy.start()
    regions = mask_ref.shape[1]
    place = lax.broadcasted_iota(jnp.int32, (8, regions), 1)
    valid = ((mask_ref[...] == 1) | (place == 0)) & (place < count_ref[0])
    valid = jnp.where(valid, 1.0, 0.0).astype(jnp.bfloat16)
    for a in range(2):
        me = lax.axis_index(axes[a])
        part, pack = parts[a], packs[a]
        shape = (regions, pack * regions)
        lane = lax.broadcasted_iota(jnp.int32, (1, shape[1]), 1)
        block = lane // (part * pack)
        odd = me % 2 == 1
        step = jnp.zeros_like(lane)
        for b, (for_even, for_odd) in enumerate(steps[a]):
            step = jnp.where(block == b, jnp.where(odd, for_odd, for_even), step)
        region = (step ^ me) * part + lane % part
        hit = lax.broadcasted_iota(jnp.int32, shape, 0) == region
        found = jnp.dot(
            valid, jnp.where(hit, 1.0, 0.0).astype(jnp.bfloat16), preferred_element_type=jnp.float32
        )
        outs[3 * a + 2][...] = jnp.where(found[:1] > 0.5, 0.0, masked_score)
    for copy in copies:
        copy.wait()


def prepare(axes, steps, parts, packs, region_mask, region_count, weights, gate_biases):
    regions = region_mask.shape[0]
    channels = weights[0].shape[-1]
    outs = []
    for pack in packs:
        outs += [
            pltpu.VMEM((channels, 5 * channels), jnp.bfloat16),
            pltpu.VMEM((1, channels), jnp.float32),
            pltpu.VMEM((1, pack * regions), jnp.float32),
        ]
    return pl.pallas_call(
        functools.partial(prepare_kernel, axes, steps, parts, packs),
        out_shape=tuple(outs),
        in_specs=[vmem, pl.BlockSpec(memory_space=pltpu.SMEM)]
        + [pl.BlockSpec(memory_space=pltpu.HBM)] * 12,
        out_specs=(vmem,) * 6,
        scratch_shapes=[pltpu.SemaphoreType.DMA((12,))],
        compiler_params=pltpu.CompilerParams(vmem_limit_bytes=16 * 2**20),
        cost_estimate=pl.CostEstimate(flops=2**20, bytes_accessed=2**20, transcendentals=0),
    )(
        region_mask.reshape(1, regions),
        region_count,
        *(pltpu.with_memory_space_constraint(w, pltpu.HBM) for w in (*weights, *gate_biases)),
    )


def attend_kernel(counts, items, pack, group, *refs):
    block_refs = refs[: len(counts)]
    weight_ref, gate_bias_ref, bias_ref, out_ref, turned_ref = refs[len(counts) :]
    channels = weight_ref.shape[0]
    head_size = channels // H
    rows = out_ref.shape[0]
    part = rows // items
    step_rows, pack_rows = group * part, pack * part
    blocks = sum(counts)
    scale = math.log2(math.e) / math.sqrt(head_size)
    head_of = lax.broadcasted_iota(jnp.int32, (1, channels), 1) // head_size
    shape = (H * pack_rows, blocks * pack_rows)
    row_item = lax.broadcasted_iota(jnp.int32, shape, 0) // part % pack
    key_item = lax.broadcasted_iota(jnp.int32, shape, 1) // part % pack
    bias = jnp.where(row_item == key_item, bias_ref[...], masked_score)

    def step(start):
        x = jnp.concatenate(
            [
                ref[pl.ds(b * rows + start, step_rows), :]
                for ref, count in zip(block_refs, counts)
                for b in range(count)
            ],
            0,
        ).astype(jnp.float32)
        centered = x - jnp.mean(x, axis=1, keepdims=True)
        variance = jnp.mean(centered * centered, axis=1, keepdims=True)
        normed = (centered * lax.rsqrt(variance + epsilon)).astype(jnp.bfloat16)
        own_products = jnp.dot(
            normed[:step_rows], weight_ref[:, : 2 * channels], preferred_element_type=jnp.float32
        )
        queries = own_products[:, :channels]
        gate = jax.nn.sigmoid(own_products[:, channels:] + gate_bias_ref[...])
        products = jnp.dot(
            normed, weight_ref[:, 2 * channels : 4 * channels], preferred_element_type=jnp.float32
        ).astype(jnp.bfloat16)
        attended = []
        for i in range(group // pack):
            at = [b * step_rows + i * pack_rows for b in range(blocks)]
            both = jnp.concatenate([products[a : a + pack_rows] for a in at], 0)
            q = queries[i * pack_rows : (i + 1) * pack_rows]
            stacked = jnp.concatenate(
                [jnp.where(head_of == h, q, 0.0) for h in range(H)], 0
            ).astype(jnp.bfloat16)
            scores = (
                lax.dot_general(
                    stacked,
                    both[:, :channels],
                    (((1,), (1,)), ((), ())),
                    preferred_element_type=jnp.float32,
                )
                * scale
                + bias
            )
            expanded = jnp.exp2(scores - jnp.max(scores, axis=1, keepdims=True))
            weights = expanded * (1.0 / jnp.sum(expanded, axis=1, keepdims=True))
            heads = jnp.dot(
                weights.astype(jnp.bfloat16), both[:, channels:], preferred_element_type=jnp.float32
            )
            picked = heads[:pack_rows]
            for h in range(1, H):
                picked = jnp.where(
                    head_of == h, heads[h * pack_rows : (h + 1) * pack_rows], picked
                )
            attended.append(picked)
        attended = jnp.concatenate(attended, 0).astype(jnp.bfloat16).astype(jnp.float32)
        gated = (gate * attended).astype(jnp.bfloat16)
        return x[:step_rows] + jnp.dot(
            gated, weight_ref[:, 4 * channels :], preferred_element_type=jnp.float32
        )

    def one_group(g, start):
        result = step(start)
        for i in range(group):
            turned_ref[pl.ds(g * group + i, part, stride=items), :] = result[
                i * part : (i + 1) * part
            ]

    if group == items:
        one_group(0, 0)
    else:

        def body(g, carry):
            one_group(g, pl.multiple_of(g * step_rows, step_rows))
            return carry

        lax.fori_loop(0, items // group, body, 0)
    out_ref[...] = turned_ref[...].astype(out_ref.dtype)


def attend(blocks, counts, items, pack, group, prepared):
    rows, channels = blocks[0].shape[0] // counts[0], blocks[0].shape[1]
    held = sum(b.size * b.dtype.itemsize for b in blocks)
    return pl.pallas_call(
        functools.partial(attend_kernel, counts, items, pack, group),
        out_shape=jax.ShapeDtypeStruct((rows, channels), jnp.bfloat16),
        in_specs=[vmem] * (len(blocks) + len(prepared)),
        out_specs=vmem,
        scratch_shapes=[pltpu.VMEM((rows, channels), jnp.float32)],
        compiler_params=pltpu.CompilerParams(vmem_limit_bytes=held + 16 * 2**20),
    )(*blocks, *prepared)


def meet(size, step):
    return [(i, i ^ step) for i in range(size)]


def body(
    pair_field,
    region_mask,
    region_count,
    row_query,
    row_key,
    row_value,
    row_gate,
    row_gate_bias,
    row_out,
    col_query,
    col_key,
    col_value,
    col_gate,
    col_gate_bias,
    col_out,
):
    tile_rows, tile_cols, channels = pair_field.shape
    dest_size = lax.axis_size("dest")
    orig_size = lax.axis_size("orig")
    regions = region_mask.shape[0]
    row_steps = list(range(dest_size))
    near = list(range(0, orig_size, 2))
    col_steps = near + [s ^ 1 for s in near]
    row_packing = packing(tile_rows, regions)
    col_packing = packing(tile_cols, regions)
    prepared = prepare(
        ("dest", "orig"),
        ([(s, s) for s in row_steps], [(s, s) for s in col_steps]),
        (tile_cols, tile_rows),
        (row_packing[0], col_packing[0]),
        region_mask,
        region_count,
        (row_query, row_gate, row_key, row_value, row_out)
        + (col_query, col_gate, col_key, col_value, col_out),
        (row_gate_bias, col_gate_bias),
    )

    tile = pair_field.reshape(tile_rows * tile_cols, channels)
    blocks = [tile] + [lax.ppermute(tile, "dest", meet(dest_size, s)) for s in row_steps[1:]]
    turned = attend(blocks, [1] * dest_size, tile_rows, *row_packing, prepared[:3])

    held = jnp.concatenate(
        [turned] + [lax.ppermute(turned, "orig", meet(orig_size, s)) for s in near[1:]], 0
    )
    other = lax.ppermute(held, "orig", meet(orig_size, 1))
    result = attend([held, other], [len(near)] * 2, tile_cols, *col_packing, prepared[3:])
    return result.reshape(tile_rows, tile_cols, channels)


def solution(mesh):
    tile = P("orig", "dest", None)
    in_specs = (tile,) + (P(),) * 14
    return jax.shard_map(body, mesh=mesh, in_specs=in_specs, out_specs=tile, check_vma=False)
```

```python
import functools
import math

import jax
import jax.numpy as jnp
from jax import lax
from jax.experimental import pallas as pl
from jax.experimental.pallas import tpu as pltpu
from jax.sharding import PartitionSpec as P

H = 4

epsilon = 1e-05
masked_score = -1e30
lanes = 128
group_rows = 1024

vmem = pl.BlockSpec(memory_space=pltpu.VMEM)


def packing(items, length):
    pack = max(p for p in range(1, items + 1) if items % p == 0 and (p == 1 or p * length <= lanes))
    group = max(
        g
        for g in range(pack, items + 1, pack)
        if items % g == 0 and (g == pack or g * length <= group_rows)
    )
    return pack, group


def prepare_kernel(axes, steps, parts, packs, mask_ref, count_ref, *refs):
    weights, gate_biases, outs, sem = refs[:10], refs[10:12], refs[12:18], refs[18]
    channels = weights[0].shape[1]
    copies = []
    for a in range(2):
        for w in range(5):
            copies.append(
                pltpu.make_async_copy(
                    weights[5 * a + w].at[0],
                    outs[3 * a].at[:, pl.ds(w * channels, channels)],
                    sem.at[len(copies)],
                )
            )
        copies.append(pltpu.make_async_copy(gate_biases[a], outs[3 * a + 1], sem.at[len(copies)]))
    for copy in copies:
        copy.start()
    regions = mask_ref.shape[1]
    place = lax.broadcasted_iota(jnp.int32, (8, regions), 1)
    valid = ((mask_ref[...] == 1) | (place == 0)) & (place < count_ref[0])
    valid = jnp.where(valid, 1.0, 0.0).astype(jnp.bfloat16)
    for a in range(2):
        me = lax.axis_index(axes[a])
        part, pack = parts[a], packs[a]
        shape = (regions, pack * regions)
        lane = lax.broadcasted_iota(jnp.int32, (1, shape[1]), 1)
        block = lane // (part * pack)
        step = jnp.zeros_like(lane)
        for b, value in enumerate(steps[a]):
            step = jnp.where(block == b, value, step)
        region = (step ^ me) * part + lane % part
        hit = lax.broadcasted_iota(jnp.int32, shape, 0) == region
        found = jnp.dot(
            valid, jnp.where(hit, 1.0, 0.0).astype(jnp.bfloat16), preferred_element_type=jnp.float32
        )
        outs[3 * a + 2][...] = jnp.where(found[:1] > 0.5, 0.0, masked_score)
    for copy in copies:
        copy.wait()


def prepare(axes, steps, parts, packs, region_mask, region_count, weights, gate_biases):
    regions = region_mask.shape[0]
    channels = weights[0].shape[-1]
    outs = []
    for pack in packs:
        outs += [
            pltpu.VMEM((channels, 5 * channels), jnp.bfloat16),
            pltpu.VMEM((1, channels), jnp.float32),
            pltpu.VMEM((1, pack * regions), jnp.float32),
        ]
    return pl.pallas_call(
        functools.partial(prepare_kernel, axes, steps, parts, packs),
        out_shape=tuple(outs),
        in_specs=[vmem, pl.BlockSpec(memory_space=pltpu.SMEM)]
        + [pl.BlockSpec(memory_space=pltpu.HBM)] * 12,
        out_specs=(vmem,) * 6,
        scratch_shapes=[pltpu.SemaphoreType.DMA((12,))],
        compiler_params=pltpu.CompilerParams(vmem_limit_bytes=16 * 2**20),
        cost_estimate=pl.CostEstimate(flops=2**20, bytes_accessed=2**20, transcendentals=0),
    )(
        region_mask.reshape(1, regions),
        region_count,
        *(pltpu.with_memory_space_constraint(w, pltpu.HBM) for w in (*weights, *gate_biases)),
    )


def attend_kernel(items, pack, group, *refs):
    *block_refs, weight_ref, gate_bias_ref, bias_ref, out_ref, turned_ref = refs
    channels = weight_ref.shape[0]
    head_size = channels // H
    rows = out_ref.shape[0]
    part = rows // items
    step_rows, pack_rows = group * part, pack * part
    places = [(ref, b) for ref in block_refs for b in range(ref.shape[0] // rows)]
    blocks = len(places)
    scale = math.log2(math.e) / math.sqrt(head_size)
    head_of = lax.broadcasted_iota(jnp.int32, (1, channels), 1) // head_size
    shape = (H * pack_rows, blocks * pack_rows)
    row_item = lax.broadcasted_iota(jnp.int32, shape, 0) // part % pack
    key_item = lax.broadcasted_iota(jnp.int32, shape, 1) // part % pack
    bias = jnp.where(row_item == key_item, bias_ref[...], masked_score)

    def step(start):
        x = jnp.concatenate(
            [ref[pl.ds(b * rows + start, step_rows), :] for ref, b in places], 0
        ).astype(jnp.float32)
        centered = x - jnp.mean(x, axis=1, keepdims=True)
        variance = jnp.mean(centered * centered, axis=1, keepdims=True)
        normed = (centered * lax.rsqrt(variance + epsilon)).astype(jnp.bfloat16)
        own_products = jnp.dot(
            normed[:step_rows], weight_ref[:, : 2 * channels], preferred_element_type=jnp.float32
        )
        queries = own_products[:, :channels]
        gate = jax.nn.sigmoid(own_products[:, channels:] + gate_bias_ref[...])
        products = jnp.dot(
            normed, weight_ref[:, 2 * channels : 4 * channels], preferred_element_type=jnp.float32
        ).astype(jnp.bfloat16)
        packs = range(group // pack)
        held = [
            jnp.concatenate(
                [products[b * step_rows + i * pack_rows :][:pack_rows] for b in range(blocks)], 0
            )
            for i in packs
        ]
        stacked = [
            jnp.concatenate(
                [
                    jnp.where(head_of == h, queries[i * pack_rows : (i + 1) * pack_rows], 0.0)
                    for h in range(H)
                ],
                0,
            ).astype(jnp.bfloat16)
            for i in packs
        ]
        scores = [
            lax.dot_general(
                stacked[i],
                held[i][:, :channels],
                (((1,), (1,)), ((), ())),
                preferred_element_type=jnp.float32,
            )
            * scale
            + bias
            for i in packs
        ]
        scores = jnp.concatenate(scores, 0)
        expanded = jnp.exp2(scores - jnp.max(scores, axis=1, keepdims=True))
        weights = (expanded * (1.0 / jnp.sum(expanded, axis=1, keepdims=True))).astype(jnp.bfloat16)
        attended = []
        for i in packs:
            heads = jnp.dot(
                weights[i * H * pack_rows : (i + 1) * H * pack_rows],
                held[i][:, channels:],
                preferred_element_type=jnp.float32,
            )
            picked = heads[:pack_rows]
            for h in range(1, H):
                picked = jnp.where(
                    head_of == h, heads[h * pack_rows : (h + 1) * pack_rows], picked
                )
            attended.append(picked)
        attended = jnp.concatenate(attended, 0).astype(jnp.bfloat16).astype(jnp.float32)
        gated = (gate * attended).astype(jnp.bfloat16)
        return x[:step_rows] + jnp.dot(
            gated, weight_ref[:, 4 * channels :], preferred_element_type=jnp.float32
        )

    def one_group(g, start):
        result = step(start)
        for i in range(group):
            turned_ref[pl.ds(g * group + i, part, stride=items), :] = result[
                i * part : (i + 1) * part
            ]

    if group == items:
        one_group(0, 0)
    else:

        def body(g, carry):
            one_group(g, pl.multiple_of(g * step_rows, step_rows))
            return carry

        lax.fori_loop(0, items // group, body, 0)
    out_ref[...] = turned_ref[...].astype(out_ref.dtype)


def attend(blocks, rows, items, packing, prepared):
    channels = blocks[0].shape[1]
    held = sum(b.size * b.dtype.itemsize for b in blocks)
    return pl.pallas_call(
        functools.partial(attend_kernel, items, *packing),
        out_shape=jax.ShapeDtypeStruct((rows, channels), jnp.bfloat16),
        in_specs=[vmem] * (len(blocks) + len(prepared)),
        out_specs=vmem,
        scratch_shapes=[pltpu.VMEM((rows, channels), jnp.float32)],
        compiler_params=pltpu.CompilerParams(vmem_limit_bytes=held + 16 * 2**20),
    )(*blocks, *prepared)


def fetch(values, orig_step, dest_step=0):
    orig_size, dest_size = lax.axis_size("orig"), lax.axis_size("dest")
    pairs = [
        (o * dest_size + d, (o ^ orig_step) * dest_size + (d ^ dest_step))
        for o in range(orig_size)
        for d in range(dest_size)
    ]
    return lax.ppermute(values, ("orig", "dest"), pairs)


def body(
    pair_field,
    region_mask,
    region_count,
    row_query,
    row_key,
    row_value,
    row_gate,
    row_gate_bias,
    row_out,
    col_query,
    col_key,
    col_value,
    col_gate,
    col_gate_bias,
    col_out,
):
    tile_rows, tile_cols, channels = pair_field.shape
    dest_size = lax.axis_size("dest")
    orig_size = lax.axis_size("orig")
    regions = region_mask.shape[0]
    row_steps = list(range(dest_size))
    chip_steps = list(range(2, orig_size, 2))
    col_steps = [0, 1] + chip_steps + [s ^ 1 for s in chip_steps]
    row_packing = packing(tile_rows, regions)
    col_packing = packing(tile_cols, regions)
    rows = tile_rows * tile_cols
    prepared = prepare(
        ("dest", "orig"),
        (row_steps, col_steps),
        (tile_cols, tile_rows),
        (row_packing[0], col_packing[0]),
        region_mask,
        region_count,
        (row_query, row_gate, row_key, row_value, row_out)
        + (col_query, col_gate, col_key, col_value, col_out),
        (row_gate_bias, col_gate_bias),
    )

    tile = pair_field.reshape(rows, channels)
    blocks = [fetch(tile, 1, s) for s in row_steps]
    turned = attend(blocks, rows, tile_rows, row_packing, prepared[:3])
    own = fetch(turned, 1)
    near = jnp.concatenate([fetch(turned, s ^ 1) for s in chip_steps], 0)
    blocks = [own, turned, near, fetch(near, 1)]
    result = attend(blocks, rows, tile_cols, col_packing, prepared[3:])
    return result.reshape(tile_rows, tile_cols, channels)


def solution(mesh):
    tile = P("orig", "dest", None)
    in_specs = (tile,) + (P(),) * 14
    return jax.shard_map(body, mesh=mesh, in_specs=in_specs, out_specs=tile, check_vma=False)
```

```python
import functools
import math

import jax
import jax.numpy as jnp
from jax import lax
from jax.experimental import pallas as pl
from jax.experimental.pallas import tpu as pltpu
from jax.sharding import PartitionSpec as P

H = 4

epsilon = 1e-05
masked_score = -1e30
lanes = 128
group_rows = 1024

vmem = pl.BlockSpec(memory_space=pltpu.VMEM)


def packing(items, length):
    pack = max(p for p in range(1, items + 1) if items % p == 0 and (p == 1 or p * length <= lanes))
    group = max(
        g
        for g in range(pack, items + 1, pack)
        if items % g == 0 and (g == pack or g * length <= group_rows)
    )
    return pack, group


def reverse(index, size):
    bits = size.bit_length() - 1
    return sum(((index >> b) & 1) << (bits - 1 - b) for b in range(bits))


def prepare_kernel(axes, sources, parts, packs, mask_ref, count_ref, *refs):
    weights, gate_biases, outs, sem = refs[:10], refs[10:12], refs[12:18], refs[18]
    channels = weights[0].shape[1]
    copies = []
    for a in range(2):
        for w in range(5):
            copies.append(
                pltpu.make_async_copy(
                    weights[5 * a + w].at[0],
                    outs[3 * a].at[:, pl.ds(w * channels, channels)],
                    sem.at[len(copies)],
                )
            )
        copies.append(pltpu.make_async_copy(gate_biases[a], outs[3 * a + 1], sem.at[len(copies)]))
    for copy in copies:
        copy.start()
    regions = mask_ref.shape[1]
    place = lax.broadcasted_iota(jnp.int32, (8, regions), 1)
    valid = ((mask_ref[...] == 1) | (place == 0)) & (place < count_ref[0])
    valid = jnp.where(valid, 1.0, 0.0).astype(jnp.bfloat16)
    for a in range(2):
        me = lax.axis_index(axes[a])
        part, pack = parts[a], packs[a]
        shape = (regions, pack * regions)
        lane = lax.broadcasted_iota(jnp.int32, (1, shape[1]), 1)
        block = lane // (part * pack)
        region = lane % part
        for b, source in enumerate(sources[a]):
            region += jnp.where(block == b, source(me) * part, 0)
        hit = lax.broadcasted_iota(jnp.int32, shape, 0) == region
        found = jnp.dot(
            valid, jnp.where(hit, 1.0, 0.0).astype(jnp.bfloat16), preferred_element_type=jnp.float32
        )
        outs[3 * a + 2][...] = jnp.where(found[:1] > 0.5, 0.0, masked_score)
    for copy in copies:
        copy.wait()


def prepare(axes, sources, parts, packs, region_mask, region_count, weights, gate_biases):
    regions = region_mask.shape[0]
    channels = weights[0].shape[-1]
    outs = []
    for pack in packs:
        outs += [
            pltpu.VMEM((channels, 5 * channels), jnp.bfloat16),
            pltpu.VMEM((1, channels), jnp.float32),
            pltpu.VMEM((1, pack * regions), jnp.float32),
        ]
    return pl.pallas_call(
        functools.partial(prepare_kernel, axes, sources, parts, packs),
        out_shape=tuple(outs),
        in_specs=[vmem, pl.BlockSpec(memory_space=pltpu.SMEM)]
        + [pl.BlockSpec(memory_space=pltpu.HBM)] * 12,
        out_specs=(vmem,) * 6,
        scratch_shapes=[pltpu.SemaphoreType.DMA((12,))],
        compiler_params=pltpu.CompilerParams(vmem_limit_bytes=16 * 2**20),
        cost_estimate=pl.CostEstimate(flops=2**20, bytes_accessed=2**20, transcendentals=0),
    )(
        region_mask.reshape(1, regions),
        region_count,
        *(pltpu.with_memory_space_constraint(w, pltpu.HBM) for w in (*weights, *gate_biases)),
    )


def attend_kernel(items, pack, group, *refs):
    *block_refs, weight_ref, gate_bias_ref, bias_ref, out_ref, turned_ref = refs
    channels = weight_ref.shape[0]
    head_size = channels // H
    rows = out_ref.shape[0]
    part = rows // items
    step_rows, pack_rows = group * part, pack * part
    places = [(ref, b) for ref in block_refs for b in range(ref.shape[0] // rows)]
    blocks = len(places)
    scale = math.log2(math.e) / math.sqrt(head_size)
    head_of = lax.broadcasted_iota(jnp.int32, (1, channels), 1) // head_size
    shape = (H * pack_rows, blocks * pack_rows)
    row_item = lax.broadcasted_iota(jnp.int32, shape, 0) // part % pack
    key_item = lax.broadcasted_iota(jnp.int32, shape, 1) // part % pack
    bias = jnp.where(row_item == key_item, bias_ref[...], masked_score)

    def step(start):
        x = jnp.concatenate(
            [ref[pl.ds(b * rows + start, step_rows), :] for ref, b in places], 0
        )
        averaging = jnp.full((channels, channels), 1.0 / channels, jnp.bfloat16)
        mean = jnp.dot(x, averaging, preferred_element_type=jnp.float32)
        x = x.astype(jnp.float32)
        centered = x - mean
        variance = jnp.mean(centered * centered, axis=1, keepdims=True)
        normed = (centered * lax.rsqrt(variance + epsilon)).astype(jnp.bfloat16)
        own_products = jnp.dot(
            normed[:step_rows], weight_ref[:, : 2 * channels], preferred_element_type=jnp.float32
        )
        queries = own_products[:, :channels]
        gate = jax.nn.sigmoid(own_products[:, channels:] + gate_bias_ref[...])
        products = jnp.dot(
            normed, weight_ref[:, 2 * channels : 4 * channels], preferred_element_type=jnp.float32
        ).astype(jnp.bfloat16)
        packs = range(group // pack)
        held = [
            jnp.concatenate(
                [products[b * step_rows + i * pack_rows :][:pack_rows] for b in range(blocks)], 0
            )
            for i in packs
        ]
        stacked = [
            jnp.concatenate(
                [
                    jnp.where(head_of == h, queries[i * pack_rows : (i + 1) * pack_rows], 0.0)
                    for h in range(H)
                ],
                0,
            ).astype(jnp.bfloat16)
            for i in packs
        ]
        scores = [
            lax.dot_general(
                stacked[i],
                held[i][:, :channels],
                (((1,), (1,)), ((), ())),
                preferred_element_type=jnp.float32,
            )
            * scale
            + bias
            for i in packs
        ]
        scores = jnp.concatenate(scores, 0)
        expanded = jnp.exp2(scores - jnp.max(scores, axis=1, keepdims=True))
        weights = (expanded * (1.0 / jnp.sum(expanded, axis=1, keepdims=True))).astype(jnp.bfloat16)
        attended = []
        for i in packs:
            heads = jnp.dot(
                weights[i * H * pack_rows : (i + 1) * H * pack_rows],
                held[i][:, channels:],
                preferred_element_type=jnp.float32,
            )
            picked = heads[:pack_rows]
            for h in range(1, H):
                picked = jnp.where(
                    head_of == h, heads[h * pack_rows : (h + 1) * pack_rows], picked
                )
            attended.append(picked)
        attended = jnp.concatenate(attended, 0).astype(jnp.bfloat16).astype(jnp.float32)
        gated = (gate * attended).astype(jnp.bfloat16)
        return x[:step_rows] + jnp.dot(
            gated, weight_ref[:, 4 * channels :], preferred_element_type=jnp.float32
        )

    def one_group(g, start):
        result = step(start)
        for i in range(group):
            turned_ref[pl.ds(g * group + i, part, stride=items), :] = result[
                i * part : (i + 1) * part
            ]

    if group == items:
        one_group(0, 0)
    else:

        def body(g, carry):
            one_group(g, pl.multiple_of(g * step_rows, step_rows))
            return carry

        lax.fori_loop(0, items // group, body, 0)
    out_ref[...] = turned_ref[...].astype(out_ref.dtype)


def attend(blocks, rows, items, packing, prepared):
    channels = blocks[0].shape[1]
    held = sum(b.size * b.dtype.itemsize for b in blocks)
    return pl.pallas_call(
        functools.partial(attend_kernel, items, *packing),
        out_shape=jax.ShapeDtypeStruct((rows, channels), jnp.bfloat16),
        in_specs=[vmem] * (len(blocks) + len(prepared)),
        out_specs=vmem,
        scratch_shapes=[pltpu.VMEM((rows, channels), jnp.float32)],
        compiler_params=pltpu.CompilerParams(vmem_limit_bytes=held + 16 * 2**20),
    )(*blocks, *prepared)


def send(values, to):
    orig_size, dest_size = lax.axis_size("orig"), lax.axis_size("dest")
    pairs = []
    for o in range(orig_size):
        for d in range(dest_size):
            far_o, far_d = to(o, d)
            pairs.append((o * dest_size + d, far_o * dest_size + far_d))
    return lax.ppermute(values, ("orig", "dest"), pairs)


def body(
    pair_field,
    region_mask,
    region_count,
    row_query,
    row_key,
    row_value,
    row_gate,
    row_gate_bias,
    row_out,
    col_query,
    col_key,
    col_value,
    col_gate,
    col_gate_bias,
    col_out,
):
    tile_rows, tile_cols, channels = pair_field.shape
    dest_size = lax.axis_size("dest")
    orig_size = lax.axis_size("orig")
    regions = region_mask.shape[0]
    row_steps = sorted(range(dest_size), key=lambda s: (s > 0, -min(s, dest_size - s), -s))
    chip_steps = list(range(2, orig_size, 2))
    col_steps = [0, 1] + chip_steps + [s ^ 1 for s in chip_steps]

    def along_dest(d, step):
        return reverse((reverse(d, dest_size) + step) % dest_size, dest_size)

    row_packing = packing(tile_rows, regions)
    col_packing = packing(tile_cols, regions)
    rows = tile_rows * tile_cols
    prepared = prepare(
        ("dest", "orig"),
        (
            [lambda d, s=s: along_dest(d, dest_size - s) for s in row_steps],
            [lambda o, s=s: o ^ s for s in col_steps],
        ),
        (tile_cols, tile_rows),
        (row_packing[0], col_packing[0]),
        region_mask,
        region_count,
        (row_query, row_gate, row_key, row_value, row_out)
        + (col_query, col_gate, col_key, col_value, col_out),
        (row_gate_bias, col_gate_bias),
    )

    tile = pair_field.reshape(rows, channels)
    blocks = [send(tile, lambda o, d: (o ^ 1, along_dest(d, s))) for s in row_steps]
    turned = attend(blocks, rows, tile_rows, row_packing, prepared[:3])
    own = send(turned, lambda o, d: (o ^ 1, d))
    near = [send(turned, lambda o, d: (o ^ s ^ 1, d)) for s in chip_steps]
    other = [send(block, lambda o, d: (o ^ 1, d)) for block in near]
    blocks = [own, turned] + near + other
    result = attend(blocks, rows, tile_cols, col_packing, prepared[3:])
    return result.reshape(tile_rows, tile_cols, channels)


def solution(mesh):
    tile = P("orig", "dest", None)
    in_specs = (tile,) + (P(),) * 14
    return jax.shard_map(body, mesh=mesh, in_specs=in_specs, out_specs=tile, check_vma=False)
```

```python
import functools
import math

import jax
import jax.numpy as jnp
from jax import lax
from jax.experimental import pallas as pl
from jax.experimental.pallas import tpu as pltpu
from jax.sharding import PartitionSpec as P

H = 4

epsilon = 1e-05
masked_score = -1e30
lanes = 128
group_rows = 1024

vmem = pl.BlockSpec(memory_space=pltpu.VMEM)


def packing(items, length):
    pack = max(p for p in range(1, items + 1) if items % p == 0 and (p == 1 or p * length <= lanes))
    group = max(
        g
        for g in range(pack, items + 1, pack)
        if items % g == 0 and (g == pack or g * length <= group_rows)
    )
    return pack, group


def reverse(index, size):
    bits = size.bit_length() - 1
    return sum(((index >> b) & 1) << (bits - 1 - b) for b in range(bits))


def prepare_kernel(axes, sources, parts, packs, mask_ref, count_ref, *refs):
    weights, gate_biases, outs, sem = refs[:10], refs[10:12], refs[12:18], refs[18]
    channels = weights[0].shape[1]
    copies = []
    for a in range(2):
        for w in range(5):
            copies.append(
                pltpu.make_async_copy(
                    weights[5 * a + w].at[0],
                    outs[3 * a].at[:, pl.ds(w * channels, channels)],
                    sem.at[len(copies)],
                )
            )
        copies.append(pltpu.make_async_copy(gate_biases[a], outs[3 * a + 1], sem.at[len(copies)]))
    for copy in copies:
        copy.start()
    regions = mask_ref.shape[1]
    place = lax.broadcasted_iota(jnp.int32, (8, regions), 1)
    valid = ((mask_ref[...] == 1) | (place == 0)) & (place < count_ref[0])
    valid = jnp.where(valid, 1.0, 0.0).astype(jnp.bfloat16)
    for a in range(2):
        me = lax.axis_index(axes[a])
        part, pack = parts[a], packs[a]
        shape = (regions, pack * regions)
        lane = lax.broadcasted_iota(jnp.int32, (1, shape[1]), 1)
        block = lane // (part * pack)
        region = lane % part
        for b, source in enumerate(sources[a]):
            region += jnp.where(block == b, source(me) * part, 0)
        hit = lax.broadcasted_iota(jnp.int32, shape, 0) == region
        found = jnp.dot(
            valid, jnp.where(hit, 1.0, 0.0).astype(jnp.bfloat16), preferred_element_type=jnp.float32
        )
        outs[3 * a + 2][...] = jnp.where(found[:1] > 0.5, 0.0, masked_score)
    for copy in copies:
        copy.wait()


def prepare(axes, sources, parts, packs, region_mask, region_count, weights, gate_biases):
    regions = region_mask.shape[0]
    channels = weights[0].shape[-1]
    outs = []
    for pack in packs:
        outs += [
            pltpu.VMEM((channels, 5 * channels), jnp.bfloat16),
            pltpu.VMEM((1, channels), jnp.float32),
            pltpu.VMEM((1, pack * regions), jnp.float32),
        ]
    return pl.pallas_call(
        functools.partial(prepare_kernel, axes, sources, parts, packs),
        out_shape=tuple(outs),
        in_specs=[vmem, pl.BlockSpec(memory_space=pltpu.SMEM)]
        + [pl.BlockSpec(memory_space=pltpu.HBM)] * 12,
        out_specs=(vmem,) * 6,
        scratch_shapes=[pltpu.SemaphoreType.DMA((12,))],
        compiler_params=pltpu.CompilerParams(vmem_limit_bytes=16 * 2**20),
        cost_estimate=pl.CostEstimate(flops=2**20, bytes_accessed=2**20, transcendentals=0),
    )(
        region_mask.reshape(1, regions),
        region_count,
        *(pltpu.with_memory_space_constraint(w, pltpu.HBM) for w in (*weights, *gate_biases)),
    )


def normalize(x):
    channels = x.shape[1]
    averaging = jnp.full((channels, channels), 1.0 / channels, jnp.bfloat16)
    mean = jnp.dot(x, averaging, preferred_element_type=jnp.float32)
    centered = x.astype(jnp.float32) - mean
    variance = jnp.mean(centered * centered, axis=1, keepdims=True)
    return (centered * lax.rsqrt(variance + epsilon)).astype(jnp.bfloat16)


def keys_and_values(normed, weight_ref):
    channels = weight_ref.shape[0]
    return jnp.dot(
        normed, weight_ref[:, 2 * channels : 4 * channels], preferred_element_type=jnp.float32
    ).astype(jnp.bfloat16)


def queries_and_gate(normed, weight_ref, gate_bias_ref):
    channels = weight_ref.shape[0]
    products = jnp.dot(normed, weight_ref[:, : 2 * channels], preferred_element_type=jnp.float32)
    return products[:, :channels], jax.nn.sigmoid(products[:, channels:] + gate_bias_ref[...])


def project_kernel(own, *refs):
    *block_refs, weight_ref, gate_bias_ref, query_ref, gate_ref, product_ref = refs
    rows, channels = block_refs[0].shape

    def keep(at, normed):
        queries, gate_ref[at] = queries_and_gate(normed, weight_ref, gate_bias_ref)
        query_ref[at] = queries.astype(jnp.bfloat16)

    if rows * len(block_refs) <= group_rows:
        normed = normalize(jnp.concatenate([ref[...] for ref in block_refs], 0))
        keep(slice(None), normed[own * rows : (own + 1) * rows])
        product_ref[...] = keys_and_values(normed, weight_ref)
        return
    chunk = math.gcd(rows, group_rows)
    for b, ref in enumerate(block_refs):

        def body(c, carry):
            at = pl.ds(pl.multiple_of(c * chunk, chunk), chunk)
            normed = normalize(ref[at])
            if b == own:
                keep(at, normed)
            to = pl.ds(pl.multiple_of(b * rows + c * chunk, chunk), chunk)
            product_ref[to] = keys_and_values(normed, weight_ref)
            return carry

        lax.fori_loop(0, rows // chunk, body, 0)


def attend_kernel(split, own, items, pack, group, *refs):
    weight_ref, gate_bias_ref, bias_ref, out_ref, turned_ref = refs[-5:]
    rows, channels = out_ref.shape
    if split:
        own_ref, query_ref, gate_ref, product_ref, *late_refs = refs[:-5]
    else:
        late_refs = refs[:-5]
        own_ref = late_refs[own]
    early = product_ref.shape[0] // rows if split else 0
    head_size = channels // H
    part = rows // items
    step_rows, pack_rows = group * part, pack * part
    blocks = early + len(late_refs)
    scale = math.log2(math.e) / math.sqrt(head_size)
    head_of = lax.broadcasted_iota(jnp.int32, (1, channels), 1) // head_size
    shape = (H * pack_rows, blocks * pack_rows)
    row_item = lax.broadcasted_iota(jnp.int32, shape, 0) // part % pack
    key_item = lax.broadcasted_iota(jnp.int32, shape, 1) // part % pack
    bias = jnp.where(row_item == key_item, bias_ref[...], masked_score)

    def step(start):
        here = pl.ds(start, step_rows)
        normed = normalize(jnp.concatenate([ref[here] for ref in late_refs], 0))
        if split:
            queries, gate = query_ref[here].astype(jnp.float32), gate_ref[here]
        else:
            queries, gate = queries_and_gate(
                normed[own * step_rows : (own + 1) * step_rows], weight_ref, gate_bias_ref
            )
        late = keys_and_values(normed, weight_ref)
        products = [product_ref[pl.ds(b * rows + start, step_rows)] for b in range(early)]
        products += [late[b * step_rows : (b + 1) * step_rows] for b in range(len(late_refs))]
        packs = range(group // pack)
        held = [
            jnp.concatenate([p[i * pack_rows : (i + 1) * pack_rows] for p in products], 0)
            for i in packs
        ]
        scores = []
        for i in packs:
            query = queries[i * pack_rows : (i + 1) * pack_rows]
            stacked = jnp.concatenate([jnp.where(head_of == h, query, 0.0) for h in range(H)], 0)
            scores.append(
                lax.dot_general(
                    stacked.astype(jnp.bfloat16),
                    held[i][:, :channels],
                    (((1,), (1,)), ((), ())),
                    preferred_element_type=jnp.float32,
                )
                * scale
                + bias
            )
        scores = jnp.concatenate(scores, 0)
        expanded = jnp.exp2(scores - jnp.max(scores, axis=1, keepdims=True))
        weights = (expanded * (1.0 / jnp.sum(expanded, axis=1, keepdims=True))).astype(jnp.bfloat16)
        attended = []
        for i in packs:
            heads = jnp.dot(
                weights[i * H * pack_rows : (i + 1) * H * pack_rows],
                held[i][:, channels:],
                preferred_element_type=jnp.float32,
            )
            picked = heads[:pack_rows]
            for h in range(1, H):
                picked = jnp.where(
                    head_of == h, heads[h * pack_rows : (h + 1) * pack_rows], picked
                )
            attended.append(picked)
        attended = jnp.concatenate(attended, 0).astype(jnp.bfloat16).astype(jnp.float32)
        gated = (gate * attended).astype(jnp.bfloat16)
        return own_ref[here].astype(jnp.float32) + jnp.dot(
            gated, weight_ref[:, 4 * channels :], preferred_element_type=jnp.float32
        )

    def one_group(g, start):
        result = step(start)
        for i in range(group):
            turned_ref[pl.ds(g * group + i, part, stride=items), :] = result[
                i * part : (i + 1) * part
            ]

    if group == items:
        one_group(0, 0)
    else:

        def body(g, carry):
            one_group(g, pl.multiple_of(g * step_rows, step_rows))
            return carry

        lax.fori_loop(0, items // group, body, 0)
    out_ref[...] = turned_ref[...].astype(out_ref.dtype)


def project(blocks, own, weights, gate_bias):
    rows, channels = blocks[0].shape
    return pl.pallas_call(
        functools.partial(project_kernel, own),
        out_shape=(
            jax.ShapeDtypeStruct((rows, channels), jnp.bfloat16),
            jax.ShapeDtypeStruct((rows, channels), jnp.float32),
            jax.ShapeDtypeStruct((len(blocks) * rows, 2 * channels), jnp.bfloat16),
        ),
        in_specs=[vmem] * (len(blocks) + 2),
        out_specs=(vmem,) * 3,
        compiler_params=pltpu.CompilerParams(
            vmem_limit_bytes=8 * len(blocks) * rows * channels + 16 * 2**20
        ),
    )(*blocks, weights, gate_bias)


def attend(early, late, own, items, packing, prepared):
    weights, gate_bias, bias = prepared
    operands = [*late, *prepared]
    if early:
        operands = [early[own], *project(early, own, weights, gate_bias), *operands]
    return pl.pallas_call(
        functools.partial(attend_kernel, bool(early), own, items, *packing),
        out_shape=jax.ShapeDtypeStruct(late[0].shape, jnp.bfloat16),
        in_specs=[vmem] * len(operands),
        out_specs=vmem,
        scratch_shapes=[pltpu.VMEM(late[0].shape, jnp.float32)],
        compiler_params=pltpu.CompilerParams(
            vmem_limit_bytes=sum(v.size * v.dtype.itemsize for v in operands) + 16 * 2**20
        ),
    )(*operands)


def shifts(size):
    return sorted(range(1, size), key=lambda s: (min(s, size - s), s))


def send(values, to):
    orig_size, dest_size = lax.axis_size("orig"), lax.axis_size("dest")
    pairs = []
    for o in range(orig_size):
        for d in range(dest_size):
            far_o, far_d = to(o, d)
            pairs.append((o * dest_size + d, far_o * dest_size + far_d))
    return lax.ppermute(values, ("orig", "dest"), pairs)


def body(
    pair_field,
    region_mask,
    region_count,
    row_query,
    row_key,
    row_value,
    row_gate,
    row_gate_bias,
    row_out,
    col_query,
    col_key,
    col_value,
    col_gate,
    col_gate_bias,
    col_out,
):
    tile_rows, tile_cols, channels = pair_field.shape
    dest_size = lax.axis_size("dest")
    orig_size = lax.axis_size("orig")
    regions = region_mask.shape[0]
    row_steps = shifts(dest_size) + [0]
    chip_steps = shifts(orig_size // 2)

    def along_dest(d, step):
        return reverse((reverse(d, dest_size) + step) % dest_size, dest_size)

    def along_orig(o, step, flip):
        return (o // 2 + step) % (orig_size // 2) * 2 + (o % 2 ^ flip)

    row_sources = [lambda d, s=s: along_dest(d, dest_size - s) for s in row_steps]
    col_sources = [lambda o: o, lambda o: o ^ 1]
    for flip in (0, 1):
        col_sources += [
            lambda o, s=s, flip=flip: along_orig(o, orig_size // 2 - s, flip) for s in chip_steps
        ]
    row_packing = packing(tile_rows, regions)
    col_packing = packing(tile_cols, regions)
    rows = tile_rows * tile_cols
    prepared = prepare(
        ("dest", "orig"),
        (row_sources, col_sources),
        (tile_cols, tile_rows),
        (row_packing[0], col_packing[0]),
        region_mask,
        region_count,
        (row_query, row_gate, row_key, row_value, row_out)
        + (col_query, col_gate, col_key, col_value, col_out),
        (row_gate_bias, col_gate_bias),
    )

    tile = pair_field.reshape(rows, channels)
    blocks = [send(tile, lambda o, d: (o ^ 1, along_dest(d, s))) for s in row_steps]
    turned = attend([], blocks, row_steps.index(0), tile_rows, row_packing, prepared[:3])
    own = send(turned, lambda o, d: (o ^ 1, d))
    near = [send(turned, lambda o, d: (along_orig(o, s, 1), d)) for s in chip_steps]
    other = [send(block, lambda o, d: (o ^ 1, d)) for block in near]
    early = [own, turned, *near, *other[:-1]]
    result = attend(early, other[-1:], 0, tile_cols, col_packing, prepared[3:])
    return result.reshape(tile_rows, tile_cols, channels)


def solution(mesh):
    tile = P("orig", "dest", None)
    in_specs = (tile,) + (P(),) * 14
    return jax.shard_map(body, mesh=mesh, in_specs=in_specs, out_specs=tile, check_vma=False)
```

```python
import functools
import math

import jax
import jax.numpy as jnp
from jax import lax
from jax.experimental import pallas as pl
from jax.experimental.pallas import tpu as pltpu
from jax.sharding import PartitionSpec as P

H = 4

epsilon = 1e-05
masked_score = -1e30
lanes = 128
group_rows = 1024

vmem = pl.BlockSpec(memory_space=pltpu.VMEM)


def packing(items, length):
    pack = max(p for p in range(1, items + 1) if items % p == 0 and (p == 1 or p * length <= lanes))
    group = max(
        g
        for g in range(pack, items + 1, pack)
        if items % g == 0 and (g == pack or g * length <= group_rows)
    )
    return pack, group


def reverse(index, size):
    bits = size.bit_length() - 1
    return sum(((index >> b) & 1) << (bits - 1 - b) for b in range(bits))


def prepare_kernel(axes, sources, parts, packs, mask_ref, count_ref, *refs):
    weights, gate_biases, outs, sem = refs[:10], refs[10:12], refs[12:18], refs[18]
    channels = weights[0].shape[1]
    copies = []
    for a in range(2):
        for w in range(5):
            copies.append(
                pltpu.make_async_copy(
                    weights[5 * a + w].at[0],
                    outs[3 * a].at[:, pl.ds(w * channels, channels)],
                    sem.at[len(copies)],
                )
            )
        copies.append(pltpu.make_async_copy(gate_biases[a], outs[3 * a + 1], sem.at[len(copies)]))
    for copy in copies:
        copy.start()
    regions = mask_ref.shape[1]
    place = lax.broadcasted_iota(jnp.int32, (8, regions), 1)
    valid = ((mask_ref[...] == 1) | (place == 0)) & (place < count_ref[0])
    valid = jnp.where(valid, 1.0, 0.0).astype(jnp.bfloat16)
    for a in range(2):
        me = lax.axis_index(axes[a])
        part, pack = parts[a], packs[a]
        shape = (regions, pack * regions)
        lane = lax.broadcasted_iota(jnp.int32, (1, shape[1]), 1)
        block = lane // (part * pack)
        region = lane % part
        for b, source in enumerate(sources[a]):
            region += jnp.where(block == b, source(me) * part, 0)
        hit = lax.broadcasted_iota(jnp.int32, shape, 0) == region
        found = jnp.dot(
            valid, jnp.where(hit, 1.0, 0.0).astype(jnp.bfloat16), preferred_element_type=jnp.float32
        )
        outs[3 * a + 2][...] = jnp.where(found[:1] > 0.5, 0.0, masked_score)
    for copy in copies:
        copy.wait()


def prepare(axes, sources, parts, packs, region_mask, region_count, weights, gate_biases):
    regions = region_mask.shape[0]
    channels = weights[0].shape[-1]
    outs = []
    for pack in packs:
        outs += [
            pltpu.VMEM((channels, 5 * channels), jnp.bfloat16),
            pltpu.VMEM((1, channels), jnp.float32),
            pltpu.VMEM((1, pack * regions), jnp.float32),
        ]
    return pl.pallas_call(
        functools.partial(prepare_kernel, axes, sources, parts, packs),
        out_shape=tuple(outs),
        in_specs=[vmem, pl.BlockSpec(memory_space=pltpu.SMEM)]
        + [pl.BlockSpec(memory_space=pltpu.HBM)] * 12,
        out_specs=(vmem,) * 6,
        scratch_shapes=[pltpu.SemaphoreType.DMA((12,))],
        compiler_params=pltpu.CompilerParams(vmem_limit_bytes=16 * 2**20),
        cost_estimate=pl.CostEstimate(flops=2**20, bytes_accessed=2**20, transcendentals=0),
    )(
        region_mask.reshape(1, regions),
        region_count,
        *(pltpu.with_memory_space_constraint(w, pltpu.HBM) for w in (*weights, *gate_biases)),
    )


def normalize(x):
    channels = x.shape[1]
    averaging = jnp.full((channels, channels), 1.0 / channels, jnp.bfloat16)
    mean = jnp.dot(x, averaging, preferred_element_type=jnp.float32)
    centered = x.astype(jnp.float32) - mean
    variance = jnp.mean(centered * centered, axis=1, keepdims=True)
    return (centered * lax.rsqrt(variance + epsilon)).astype(jnp.bfloat16)


def keys_and_values(normed, weight_ref):
    channels = weight_ref.shape[0]
    return jnp.dot(
        normed, weight_ref[:, 2 * channels : 4 * channels], preferred_element_type=jnp.float32
    ).astype(jnp.bfloat16)


def queries_and_gate(normed, weight_ref, gate_bias_ref):
    channels = weight_ref.shape[0]
    products = jnp.dot(normed, weight_ref[:, : 2 * channels], preferred_element_type=jnp.float32)
    return products[:, :channels], jax.nn.sigmoid(products[:, channels:] + gate_bias_ref[...])


def project_kernel(own, *refs):
    *block_refs, weight_ref, gate_bias_ref, query_ref, gate_ref, product_ref = refs
    rows = query_ref.shape[0]
    normed = normalize(jnp.concatenate([ref[...] for ref in block_refs], 0))
    queries, gate_ref[...] = queries_and_gate(
        normed[own * rows : (own + 1) * rows], weight_ref, gate_bias_ref
    )
    query_ref[...] = queries.astype(jnp.bfloat16)
    product_ref[...] = keys_and_values(normed, weight_ref)


def attend_kernel(split, own, items, pack, group, *refs):
    weight_ref, gate_bias_ref, bias_ref, out_ref, turned_ref = refs[-5:]
    rows, channels = out_ref.shape
    if split:
        own_ref, query_ref, gate_ref, product_ref, *late_refs = refs[:-5]
    else:
        late_refs = refs[:-5]
        own_ref = late_refs[own]
    early = product_ref.shape[0] // rows if split else 0
    head_size = channels // H
    part = rows // items
    step_rows, pack_rows = group * part, pack * part
    blocks = early + len(late_refs)
    scale = math.log2(math.e) / math.sqrt(head_size)
    head_of = lax.broadcasted_iota(jnp.int32, (1, channels), 1) // head_size
    shape = (H * pack_rows, blocks * pack_rows)
    row_item = lax.broadcasted_iota(jnp.int32, shape, 0) // part % pack
    key_item = lax.broadcasted_iota(jnp.int32, shape, 1) // part % pack
    bias = jnp.where(row_item == key_item, bias_ref[...], masked_score)

    def step(start):
        here = pl.ds(start, step_rows)
        normed = normalize(jnp.concatenate([ref[here] for ref in late_refs], 0))
        if split:
            queries, gate = query_ref[here].astype(jnp.float32), gate_ref[here]
        else:
            queries, gate = queries_and_gate(
                normed[own * step_rows : (own + 1) * step_rows], weight_ref, gate_bias_ref
            )
        late = keys_and_values(normed, weight_ref)
        products = [product_ref[pl.ds(b * rows + start, step_rows)] for b in range(early)]
        products += [late[b * step_rows : (b + 1) * step_rows] for b in range(len(late_refs))]
        packs = range(group // pack)
        held = [
            jnp.concatenate([p[i * pack_rows : (i + 1) * pack_rows] for p in products], 0)
            for i in packs
        ]
        scores = []
        for i in packs:
            query = queries[i * pack_rows : (i + 1) * pack_rows]
            stacked = jnp.concatenate([jnp.where(head_of == h, query, 0.0) for h in range(H)], 0)
            scores.append(
                lax.dot_general(
                    stacked.astype(jnp.bfloat16),
                    held[i][:, :channels],
                    (((1,), (1,)), ((), ())),
                    preferred_element_type=jnp.float32,
                )
                * scale
                + bias
            )
        scores = jnp.concatenate(scores, 0)
        expanded = jnp.exp2(scores - jnp.max(scores, axis=1, keepdims=True))
        weights = (expanded * (1.0 / jnp.sum(expanded, axis=1, keepdims=True))).astype(jnp.bfloat16)
        attended = []
        for i in packs:
            heads = jnp.dot(
                weights[i * H * pack_rows : (i + 1) * H * pack_rows],
                held[i][:, channels:],
                preferred_element_type=jnp.float32,
            )
            picked = heads[:pack_rows]
            for h in range(1, H):
                picked = jnp.where(
                    head_of == h, heads[h * pack_rows : (h + 1) * pack_rows], picked
                )
            attended.append(picked)
        attended = jnp.concatenate(attended, 0).astype(jnp.bfloat16).astype(jnp.float32)
        gated = (gate * attended).astype(jnp.bfloat16)
        return own_ref[here].astype(jnp.float32) + jnp.dot(
            gated, weight_ref[:, 4 * channels :], preferred_element_type=jnp.float32
        )

    def one_group(g, start):
        result = step(start)
        for i in range(group):
            turned_ref[pl.ds(g * group + i, part, stride=items), :] = result[
                i * part : (i + 1) * part
            ]

    if group == items:
        one_group(0, 0)
    else:

        def body(g, carry):
            one_group(g, pl.multiple_of(g * step_rows, step_rows))
            return carry

        lax.fori_loop(0, items // group, body, 0)
    out_ref[...] = turned_ref[...].astype(out_ref.dtype)


def project(blocks, own, weights, gate_bias):
    rows, channels = blocks[0].shape
    return pl.pallas_call(
        functools.partial(project_kernel, own),
        out_shape=(
            jax.ShapeDtypeStruct((rows, channels), jnp.bfloat16),
            jax.ShapeDtypeStruct((rows, channels), jnp.float32),
            jax.ShapeDtypeStruct((len(blocks) * rows, 2 * channels), jnp.bfloat16),
        ),
        in_specs=[vmem] * (len(blocks) + 2),
        out_specs=(vmem,) * 3,
        compiler_params=pltpu.CompilerParams(
            vmem_limit_bytes=8 * len(blocks) * rows * channels + 16 * 2**20
        ),
    )(*blocks, weights, gate_bias)


def attend(early, late, own, items, packing, prepared):
    weights, gate_bias, bias = prepared
    operands = [*late, *prepared]
    if early:
        operands = [early[own], *project(early, own, weights, gate_bias), *operands]
    return pl.pallas_call(
        functools.partial(attend_kernel, bool(early), own, items, *packing),
        out_shape=jax.ShapeDtypeStruct(late[0].shape, jnp.bfloat16),
        in_specs=[vmem] * len(operands),
        out_specs=vmem,
        scratch_shapes=[pltpu.VMEM(late[0].shape, jnp.float32)],
        compiler_params=pltpu.CompilerParams(
            vmem_limit_bytes=sum(v.size * v.dtype.itemsize for v in operands) + 16 * 2**20
        ),
    )(*operands)


def shifts(size):
    return sorted(range(1, size), key=lambda s: (min(s, size - s), s))


def send(values, to):
    orig_size, dest_size = lax.axis_size("orig"), lax.axis_size("dest")
    pairs = []
    for o in range(orig_size):
        for d in range(dest_size):
            far_o, far_d = to(o, d)
            pairs.append((o * dest_size + d, far_o * dest_size + far_d))
    return lax.ppermute(values, ("orig", "dest"), pairs)


def body(
    pair_field,
    region_mask,
    region_count,
    row_query,
    row_key,
    row_value,
    row_gate,
    row_gate_bias,
    row_out,
    col_query,
    col_key,
    col_value,
    col_gate,
    col_gate_bias,
    col_out,
):
    tile_rows, tile_cols, channels = pair_field.shape
    dest_size = lax.axis_size("dest")
    orig_size = lax.axis_size("orig")
    regions = region_mask.shape[0]
    row_steps = shifts(dest_size) + [0]
    chip_steps = shifts(orig_size // 2)

    def along_dest(d, step):
        return reverse((reverse(d, dest_size) + step) % dest_size, dest_size)

    def along_orig(o, step, flip):
        return (o // 2 + step) % (orig_size // 2) * 2 + (o % 2 ^ flip)

    row_sources = [lambda d, s=s: along_dest(d, dest_size - s) for s in row_steps]
    col_sources = [lambda o: o, lambda o: o ^ 1]
    for flip in (0, 1):
        col_sources += [
            lambda o, s=s, flip=flip: along_orig(o, orig_size // 2 - s, flip) for s in chip_steps
        ]
    row_packing = packing(tile_rows, regions)
    col_packing = packing(tile_cols, regions)
    rows = tile_rows * tile_cols
    prepared = prepare(
        ("dest", "orig"),
        (row_sources, col_sources),
        (tile_cols, tile_rows),
        (row_packing[0], col_packing[0]),
        region_mask,
        region_count,
        (row_query, row_gate, row_key, row_value, row_out)
        + (col_query, col_gate, col_key, col_value, col_out),
        (row_gate_bias, col_gate_bias),
    )

    tile = pair_field.reshape(rows, channels)
    blocks = [send(tile, lambda o, d: (o ^ 1, along_dest(d, s))) for s in row_steps]
    turned = attend([], blocks, row_steps.index(0), tile_rows, row_packing, prepared[:3])
    own = send(turned, lambda o, d: (o ^ 1, d))
    near = [send(turned, lambda o, d: (along_orig(o, s, 1), d)) for s in chip_steps]
    other = [send(block, lambda o, d: (o ^ 1, d)) for block in near]
    blocks = [own, turned, *near, *other]
    early = len(blocks) - 1 if (len(blocks) - 1) * rows <= group_rows else 0
    result = attend(blocks[:early], blocks[early:], 0, tile_cols, col_packing, prepared[3:])
    return result.reshape(tile_rows, tile_cols, channels)


def solution(mesh):
    tile = P("orig", "dest", None)
    in_specs = (tile,) + (P(),) * 14
    return jax.shard_map(body, mesh=mesh, in_specs=in_specs, out_specs=tile, check_vma=False)
```

```python
import functools
import math

import jax
import jax.numpy as jnp
from jax import lax
from jax.experimental import pallas as pl
from jax.experimental.pallas import tpu as pltpu
from jax.sharding import PartitionSpec as P

H = 4

epsilon = 1e-05
masked_score = -1e30
lanes = 128
group_rows = 1024

vmem = pl.BlockSpec(memory_space=pltpu.VMEM)


def packing(items, length):
    pack = max(p for p in range(1, items + 1) if items % p == 0 and (p == 1 or p * length <= lanes))
    group = max(
        g
        for g in range(pack, items + 1, pack)
        if items % g == 0 and (g == pack or g * length <= group_rows)
    )
    return pack, group


def reverse(index, size):
    bits = size.bit_length() - 1
    return sum(((index >> b) & 1) << (bits - 1 - b) for b in range(bits))


def prepare_kernel(axes, sources, parts, packs, mask_ref, count_ref, *refs):
    weights, gate_biases, outs, sem = refs[:10], refs[10:12], refs[12:18], refs[18]
    channels = weights[0].shape[1]
    copies = []
    for a in range(2):
        for w in range(5):
            copies.append(
                pltpu.make_async_copy(
                    weights[5 * a + w].at[0],
                    outs[3 * a].at[:, pl.ds(w * channels, channels)],
                    sem.at[len(copies)],
                )
            )
        copies.append(pltpu.make_async_copy(gate_biases[a], outs[3 * a + 1], sem.at[len(copies)]))
    for copy in copies:
        copy.start()
    regions = mask_ref.shape[1]
    place = lax.broadcasted_iota(jnp.int32, (8, regions), 1)
    valid = ((mask_ref[...] == 1) | (place == 0)) & (place < count_ref[0])
    valid = jnp.where(valid, 1.0, 0.0).astype(jnp.bfloat16)
    for a in range(2):
        me = lax.axis_index(axes[a])
        part, pack = parts[a], packs[a]
        shape = (regions, pack * regions)
        lane = lax.broadcasted_iota(jnp.int32, (1, shape[1]), 1)
        block = lane // (part * pack)
        region = lane % part
        for b, source in enumerate(sources[a]):
            region += jnp.where(block == b, source(me) * part, 0)
        hit = lax.broadcasted_iota(jnp.int32, shape, 0) == region
        found = jnp.dot(
            valid, jnp.where(hit, 1.0, 0.0).astype(jnp.bfloat16), preferred_element_type=jnp.float32
        )
        outs[3 * a + 2][...] = jnp.where(found[:1] > 0.5, 0.0, masked_score)
    for copy in copies:
        copy.wait()


def prepare(axes, sources, parts, packs, region_mask, region_count, weights, gate_biases):
    regions = region_mask.shape[0]
    channels = weights[0].shape[-1]
    outs = []
    for pack in packs:
        outs += [
            pltpu.VMEM((channels, 5 * channels), jnp.bfloat16),
            pltpu.VMEM((1, channels), jnp.float32),
            pltpu.VMEM((1, pack * regions), jnp.float32),
        ]
    return pl.pallas_call(
        functools.partial(prepare_kernel, axes, sources, parts, packs),
        out_shape=tuple(outs),
        in_specs=[vmem, pl.BlockSpec(memory_space=pltpu.SMEM)]
        + [pl.BlockSpec(memory_space=pltpu.HBM)] * 12,
        out_specs=(vmem,) * 6,
        scratch_shapes=[pltpu.SemaphoreType.DMA((12,))],
        compiler_params=pltpu.CompilerParams(vmem_limit_bytes=16 * 2**20),
        cost_estimate=pl.CostEstimate(flops=2**20, bytes_accessed=2**20, transcendentals=0),
    )(
        region_mask.reshape(1, regions),
        region_count,
        *(pltpu.with_memory_space_constraint(w, pltpu.HBM) for w in (*weights, *gate_biases)),
    )


def normalize(x):
    channels = x.shape[1]
    averaging = jnp.full((channels, channels), 1.0 / channels, jnp.bfloat16)
    mean = jnp.dot(x, averaging, preferred_element_type=jnp.float32)
    centered = x.astype(jnp.float32) - mean
    variance = jnp.mean(centered * centered, axis=1, keepdims=True)
    return (centered * lax.rsqrt(variance + epsilon)).astype(jnp.bfloat16)


def keys_and_values(normed, weight_ref):
    channels = weight_ref.shape[0]
    return tuple(
        jnp.dot(
            normed, weight_ref[:, w * channels : (w + 1) * channels], preferred_element_type=jnp.float32
        ).astype(jnp.bfloat16)
        for w in (2, 3)
    )


def queries_and_gate(normed, weight_ref, gate_bias_ref):
    channels = weight_ref.shape[0]
    products = jnp.dot(normed, weight_ref[:, : 2 * channels], preferred_element_type=jnp.float32)
    return products[:, :channels], jax.nn.sigmoid(products[:, channels:] + gate_bias_ref[...])


def project_kernel(own, *refs):
    *block_refs, weight_ref, gate_bias_ref, query_ref, gate_ref, key_ref, value_ref = refs
    rows = query_ref.shape[0]
    normed = normalize(jnp.concatenate([ref[...] for ref in block_refs], 0))
    queries, gate_ref[...] = queries_and_gate(
        normed[own * rows : (own + 1) * rows], weight_ref, gate_bias_ref
    )
    query_ref[...] = queries.astype(jnp.bfloat16)
    key_ref[...], value_ref[...] = keys_and_values(normed, weight_ref)


def attend_kernel(split, own, items, pack, group, *refs):
    weight_ref, gate_bias_ref, bias_ref, out_ref, turned_ref = refs[-5:]
    rows, channels = out_ref.shape
    if split:
        own_ref, query_ref, gate_ref, key_ref, value_ref, *late_refs = refs[:-5]
    else:
        late_refs = refs[:-5]
        own_ref = late_refs[own]
    early = key_ref.shape[0] // rows if split else 0
    head_size = channels // H
    part = rows // items
    step_rows, pack_rows = group * part, pack * part
    blocks = early + len(late_refs)
    scale = math.log2(math.e) / math.sqrt(head_size)
    head_of = lax.broadcasted_iota(jnp.int32, (1, channels), 1) // head_size
    shape = (H * pack_rows, blocks * pack_rows)
    row_item = lax.broadcasted_iota(jnp.int32, shape, 0) // part % pack
    key_item = lax.broadcasted_iota(jnp.int32, shape, 1) // part % pack
    bias = jnp.where(row_item == key_item, bias_ref[...], masked_score)

    def step(start):
        here = pl.ds(start, step_rows)
        normed = normalize(jnp.concatenate([ref[here] for ref in late_refs], 0))
        if split:
            queries, gate = query_ref[here].astype(jnp.float32), gate_ref[here]
        else:
            queries, gate = queries_and_gate(
                normed[own * step_rows : (own + 1) * step_rows], weight_ref, gate_bias_ref
            )
        late_keys, late_values = keys_and_values(normed, weight_ref)
        packs = range(group // pack)

        def by_pack(early_ref, late):
            products = [early_ref[pl.ds(b * rows + start, step_rows)] for b in range(early)]
            products += [
                late[b * step_rows : (b + 1) * step_rows] for b in range(len(late_refs))
            ]
            return [
                jnp.concatenate([p[i * pack_rows : (i + 1) * pack_rows] for p in products], 0)
                for i in packs
            ]

        keys = by_pack(key_ref if split else None, late_keys)
        values = by_pack(value_ref if split else None, late_values)
        scores = []
        for i in packs:
            query = queries[i * pack_rows : (i + 1) * pack_rows]
            stacked = jnp.concatenate([jnp.where(head_of == h, query, 0.0) for h in range(H)], 0)
            scores.append(
                lax.dot_general(
                    stacked.astype(jnp.bfloat16),
                    keys[i],
                    (((1,), (1,)), ((), ())),
                    preferred_element_type=jnp.float32,
                )
                * scale
                + bias
            )
        scores = jnp.concatenate(scores, 0)
        expanded = jnp.exp2(scores - jnp.max(scores, axis=1, keepdims=True))
        share = 1.0 / jnp.sum(expanded, axis=1, keepdims=True)
        weights = expanded.astype(jnp.bfloat16)
        attended = []
        for i in packs:
            at = slice(i * H * pack_rows, (i + 1) * H * pack_rows)
            heads = jnp.dot(weights[at], values[i], preferred_element_type=jnp.float32) * share[at]
            picked = heads[:pack_rows]
            for h in range(1, H):
                picked = jnp.where(
                    head_of == h, heads[h * pack_rows : (h + 1) * pack_rows], picked
                )
            attended.append(picked)
        attended = jnp.concatenate(attended, 0).astype(jnp.bfloat16).astype(jnp.float32)
        gated = (gate * attended).astype(jnp.bfloat16)
        return own_ref[here].astype(jnp.float32) + jnp.dot(
            gated, weight_ref[:, 4 * channels :], preferred_element_type=jnp.float32
        )

    def one_group(g, start):
        result = step(start)
        for i in range(group):
            turned_ref[pl.ds(g * group + i, part, stride=items), :] = result[
                i * part : (i + 1) * part
            ]

    if group == items:
        one_group(0, 0)
    else:

        def body(g, carry):
            one_group(g, pl.multiple_of(g * step_rows, step_rows))
            return carry

        lax.fori_loop(0, items // group, body, 0)
    out_ref[...] = turned_ref[...].astype(out_ref.dtype)


def project(blocks, own, weights, gate_bias):
    rows, channels = blocks[0].shape
    return pl.pallas_call(
        functools.partial(project_kernel, own),
        out_shape=(
            jax.ShapeDtypeStruct((rows, channels), jnp.bfloat16),
            jax.ShapeDtypeStruct((rows, channels), jnp.float32),
            jax.ShapeDtypeStruct((len(blocks) * rows, channels), jnp.bfloat16),
            jax.ShapeDtypeStruct((len(blocks) * rows, channels), jnp.bfloat16),
        ),
        in_specs=[vmem] * (len(blocks) + 2),
        out_specs=(vmem,) * 4,
        compiler_params=pltpu.CompilerParams(
            vmem_limit_bytes=8 * len(blocks) * rows * channels + 16 * 2**20
        ),
    )(*blocks, weights, gate_bias)


def attend(early, late, own, items, packing, prepared):
    weights, gate_bias, bias = prepared
    operands = [*late, *prepared]
    if early:
        operands = [early[own], *project(early, own, weights, gate_bias), *operands]
    return pl.pallas_call(
        functools.partial(attend_kernel, bool(early), own, items, *packing),
        out_shape=jax.ShapeDtypeStruct(late[0].shape, jnp.bfloat16),
        in_specs=[vmem] * len(operands),
        out_specs=vmem,
        scratch_shapes=[pltpu.VMEM(late[0].shape, jnp.float32)],
        compiler_params=pltpu.CompilerParams(
            vmem_limit_bytes=sum(v.size * v.dtype.itemsize for v in operands) + 16 * 2**20
        ),
    )(*operands)


def shifts(size):
    return sorted(range(1, size), key=lambda s: (min(s, size - s), s))


def send(values, to):
    orig_size, dest_size = lax.axis_size("orig"), lax.axis_size("dest")
    pairs = []
    for o in range(orig_size):
        for d in range(dest_size):
            far_o, far_d = to(o, d)
            pairs.append((o * dest_size + d, far_o * dest_size + far_d))
    return lax.ppermute(values, ("orig", "dest"), pairs)


def body(
    pair_field,
    region_mask,
    region_count,
    row_query,
    row_key,
    row_value,
    row_gate,
    row_gate_bias,
    row_out,
    col_query,
    col_key,
    col_value,
    col_gate,
    col_gate_bias,
    col_out,
):
    tile_rows, tile_cols, channels = pair_field.shape
    dest_size = lax.axis_size("dest")
    orig_size = lax.axis_size("orig")
    regions = region_mask.shape[0]
    row_steps = shifts(dest_size) + [0]
    chip_steps = shifts(orig_size // 2)

    def along_dest(d, step):
        return reverse((reverse(d, dest_size) + step) % dest_size, dest_size)

    def along_orig(o, step, flip):
        return (o // 2 + step) % (orig_size // 2) * 2 + (o % 2 ^ flip)

    row_sources = [lambda d, s=s: along_dest(d, dest_size - s) for s in row_steps]
    col_sources = [lambda o: o, lambda o: o ^ 1]
    for flip in (0, 1):
        col_sources += [
            lambda o, s=s, flip=flip: along_orig(o, orig_size // 2 - s, flip) for s in chip_steps
        ]
    row_packing = packing(tile_rows, regions)
    col_packing = packing(tile_cols, regions)
    rows = tile_rows * tile_cols
    prepared = prepare(
        ("dest", "orig"),
        (row_sources, col_sources),
        (tile_cols, tile_rows),
        (row_packing[0], col_packing[0]),
        region_mask,
        region_count,
        (row_query, row_gate, row_key, row_value, row_out)
        + (col_query, col_gate, col_key, col_value, col_out),
        (row_gate_bias, col_gate_bias),
    )

    tile = pair_field.reshape(rows, channels)
    blocks = [send(tile, lambda o, d: (o ^ 1, along_dest(d, s))) for s in row_steps]
    turned = attend([], blocks, row_steps.index(0), tile_rows, row_packing, prepared[:3])
    own = send(turned, lambda o, d: (o ^ 1, d))
    near = [send(turned, lambda o, d: (along_orig(o, s, 1), d)) for s in chip_steps]
    other = [send(block, lambda o, d: (o ^ 1, d)) for block in near]
    blocks = [own, turned, *near, *other]
    early = len(blocks) - 1 if (len(blocks) - 1) * rows <= group_rows else 0
    result = attend(blocks[:early], blocks[early:], 0, tile_cols, col_packing, prepared[3:])
    return result.reshape(tile_rows, tile_cols, channels)


def solution(mesh):
    tile = P("orig", "dest", None)
    in_specs = (tile,) + (P(),) * 14
    return jax.shard_map(body, mesh=mesh, in_specs=in_specs, out_specs=tile, check_vma=False)
```

```python
import functools
import math

import jax
import jax.numpy as jnp
from jax import lax
from jax.experimental import pallas as pl
from jax.experimental.pallas import tpu as pltpu
from jax.sharding import PartitionSpec as P

H = 4

epsilon = 1e-05
masked_score = -1e30
lanes = 128
group_rows = 1024

vmem = pl.BlockSpec(memory_space=pltpu.VMEM)


def packing(items, length):
    pack = max(p for p in range(1, items + 1) if items % p == 0 and (p == 1 or p * length <= lanes))
    group = max(
        g
        for g in range(pack, items + 1, pack)
        if items % g == 0 and (g == pack or g * length <= group_rows)
    )
    return pack, group


def reverse(index, size):
    bits = size.bit_length() - 1
    return sum(((index >> b) & 1) << (bits - 1 - b) for b in range(bits))


def prepare_kernel(axes, sources, parts, packs, mask_ref, count_ref, *refs):
    weights, gate_biases, outs, sem = refs[:10], refs[10:12], refs[12:18], refs[18]
    channels = weights[0].shape[1]
    copies = []
    for a in range(2):
        for w in range(5):
            copies.append(
                pltpu.make_async_copy(
                    weights[5 * a + w].at[0],
                    outs[3 * a].at[:, pl.ds(w * channels, channels)],
                    sem.at[len(copies)],
                )
            )
        copies.append(pltpu.make_async_copy(gate_biases[a], outs[3 * a + 1], sem.at[len(copies)]))
    for copy in copies:
        copy.start()
    regions = mask_ref.shape[1]
    place = lax.broadcasted_iota(jnp.int32, (8, regions), 1)
    valid = ((mask_ref[...] == 1) | (place == 0)) & (place < count_ref[0])
    valid = jnp.where(valid, 1.0, 0.0).astype(jnp.bfloat16)
    for a in range(2):
        me = lax.axis_index(axes[a])
        part, pack = parts[a], packs[a]
        shape = (regions, pack * regions)
        lane = lax.broadcasted_iota(jnp.int32, (1, shape[1]), 1)
        block = lane // (part * pack)
        region = lane % part
        for b, source in enumerate(sources[a]):
            region += jnp.where(block == b, source(me) * part, 0)
        hit = lax.broadcasted_iota(jnp.int32, shape, 0) == region
        found = jnp.dot(
            valid, jnp.where(hit, 1.0, 0.0).astype(jnp.bfloat16), preferred_element_type=jnp.float32
        )
        outs[3 * a + 2][...] = jnp.where(found[:1] > 0.5, 0.0, masked_score)
    for copy in copies:
        copy.wait()


def prepare(axes, sources, parts, packs, region_mask, region_count, weights, gate_biases):
    regions = region_mask.shape[0]
    channels = weights[0].shape[-1]
    outs = []
    for pack in packs:
        outs += [
            pltpu.VMEM((channels, 5 * channels), jnp.bfloat16),
            pltpu.VMEM((1, channels), jnp.float32),
            pltpu.VMEM((1, pack * regions), jnp.float32),
        ]
    return pl.pallas_call(
        functools.partial(prepare_kernel, axes, sources, parts, packs),
        out_shape=tuple(outs),
        in_specs=[vmem, pl.BlockSpec(memory_space=pltpu.SMEM)]
        + [pl.BlockSpec(memory_space=pltpu.HBM)] * 12,
        out_specs=(vmem,) * 6,
        scratch_shapes=[pltpu.SemaphoreType.DMA((12,))],
        compiler_params=pltpu.CompilerParams(vmem_limit_bytes=16 * 2**20),
        cost_estimate=pl.CostEstimate(flops=2**20, bytes_accessed=2**20, transcendentals=0),
    )(
        region_mask.reshape(1, regions),
        region_count,
        *(pltpu.with_memory_space_constraint(w, pltpu.HBM) for w in (*weights, *gate_biases)),
    )


def normalize(x):
    channels = x.shape[1]
    averaging = jnp.full((channels, channels), 1.0 / channels, jnp.bfloat16)
    mean = jnp.dot(x, averaging, preferred_element_type=jnp.float32)
    centered = x.astype(jnp.float32) - mean
    variance = jnp.mean(centered * centered, axis=1, keepdims=True)
    return (centered * lax.rsqrt(variance + epsilon)).astype(jnp.bfloat16)


def keys_and_values(normed, weight_ref):
    channels = weight_ref.shape[0]
    return tuple(
        jnp.dot(
            normed, weight_ref[:, w * channels : (w + 1) * channels], preferred_element_type=jnp.float32
        ).astype(jnp.bfloat16)
        for w in (2, 3)
    )


def queries_and_gate(normed, weight_ref, gate_bias_ref):
    channels = weight_ref.shape[0]
    products = jnp.dot(normed, weight_ref[:, : 2 * channels], preferred_element_type=jnp.float32)
    return products[:, :channels], jax.nn.sigmoid(products[:, channels:] + gate_bias_ref[...])


def project_kernel(own, *refs):
    *block_refs, weight_ref, gate_bias_ref, query_ref, gate_ref, key_ref, value_ref = refs
    rows = query_ref.shape[0]
    normed = normalize(jnp.concatenate([ref[...] for ref in block_refs], 0))
    queries, gate_ref[...] = queries_and_gate(
        normed[own * rows : (own + 1) * rows], weight_ref, gate_bias_ref
    )
    query_ref[...] = queries.astype(jnp.bfloat16)
    key_ref[...], value_ref[...] = keys_and_values(normed, weight_ref)


def attend_kernel(split, own, items, pack, group, *refs):
    weight_ref, gate_bias_ref, bias_ref, out_ref, turned_ref = refs[-5:]
    rows, channels = out_ref.shape
    if split:
        own_ref, query_ref, gate_ref, key_ref, value_ref, *late_refs = refs[:-5]
    else:
        late_refs = refs[:-5]
        own_ref = late_refs[own]
    early = key_ref.shape[0] // rows if split else 0
    head_size = channels // H
    part = rows // items
    step_rows, pack_rows = group * part, pack * part
    blocks = early + len(late_refs)
    scale = math.log2(math.e) / math.sqrt(head_size)
    head_of = lax.broadcasted_iota(jnp.int32, (1, channels), 1) // head_size
    shape = (H * pack_rows, blocks * pack_rows)
    row_item = lax.broadcasted_iota(jnp.int32, shape, 0) // part % pack
    key_item = lax.broadcasted_iota(jnp.int32, shape, 1) // part % pack
    bias = jnp.where(row_item == key_item, bias_ref[...], masked_score)

    def step(start):
        here = pl.ds(start, step_rows)
        normed = normalize(jnp.concatenate([ref[here] for ref in late_refs], 0))
        if split:
            queries, gate = query_ref[here].astype(jnp.float32), gate_ref[here]
        else:
            queries, gate = queries_and_gate(
                normed[own * step_rows : (own + 1) * step_rows], weight_ref, gate_bias_ref
            )
        late_keys, late_values = keys_and_values(normed, weight_ref)
        packs = range(group // pack)

        def by_pack(early_ref, late):
            products = [early_ref[pl.ds(b * rows + start, step_rows)] for b in range(early)]
            products += [
                late[b * step_rows : (b + 1) * step_rows] for b in range(len(late_refs))
            ]
            return [
                jnp.concatenate([p[i * pack_rows : (i + 1) * pack_rows] for p in products], 0)
                for i in packs
            ]

        keys = by_pack(key_ref if split else None, late_keys)
        values = by_pack(value_ref if split else None, late_values)
        scores = []
        for i in packs:
            query = queries[i * pack_rows : (i + 1) * pack_rows]
            stacked = jnp.concatenate([jnp.where(head_of == h, query, 0.0) for h in range(H)], 0)
            scores.append(
                lax.dot_general(
                    stacked.astype(jnp.bfloat16),
                    keys[i],
                    (((1,), (1,)), ((), ())),
                    preferred_element_type=jnp.float32,
                )
                * scale
                + bias
            )
        scores = jnp.concatenate(scores, 0)
        expanded = jnp.exp2(scores - jnp.max(scores, axis=1, keepdims=True))
        weights = (expanded * (1.0 / jnp.sum(expanded, axis=1, keepdims=True))).astype(jnp.bfloat16)
        attended = []
        for i in packs:
            at = slice(i * H * pack_rows, (i + 1) * H * pack_rows)
            heads = jnp.dot(weights[at], values[i], preferred_element_type=jnp.float32)
            picked = heads[:pack_rows]
            for h in range(1, H):
                picked = jnp.where(
                    head_of == h, heads[h * pack_rows : (h + 1) * pack_rows], picked
                )
            attended.append(picked)
        attended = jnp.concatenate(attended, 0).astype(jnp.bfloat16).astype(jnp.float32)
        gated = (gate * attended).astype(jnp.bfloat16)
        return own_ref[here].astype(jnp.float32) + jnp.dot(
            gated, weight_ref[:, 4 * channels :], preferred_element_type=jnp.float32
        )

    def one_group(g, start):
        result = step(start)
        for i in range(group):
            turned_ref[pl.ds(g * group + i, part, stride=items), :] = result[
                i * part : (i + 1) * part
            ]

    if group == items:
        one_group(0, 0)
    else:

        def body(g, carry):
            one_group(g, pl.multiple_of(g * step_rows, step_rows))
            return carry

        lax.fori_loop(0, items // group, body, 0)
    out_ref[...] = turned_ref[...].astype(out_ref.dtype)


def project(blocks, own, weights, gate_bias):
    rows, channels = blocks[0].shape
    return pl.pallas_call(
        functools.partial(project_kernel, own),
        out_shape=(
            jax.ShapeDtypeStruct((rows, channels), jnp.bfloat16),
            jax.ShapeDtypeStruct((rows, channels), jnp.float32),
            jax.ShapeDtypeStruct((len(blocks) * rows, channels), jnp.bfloat16),
            jax.ShapeDtypeStruct((len(blocks) * rows, channels), jnp.bfloat16),
        ),
        in_specs=[vmem] * (len(blocks) + 2),
        out_specs=(vmem,) * 4,
        compiler_params=pltpu.CompilerParams(
            vmem_limit_bytes=8 * len(blocks) * rows * channels + 16 * 2**20
        ),
    )(*blocks, weights, gate_bias)


def attend(early, late, own, items, packing, prepared):
    weights, gate_bias, bias = prepared
    operands = [*late, *prepared]
    if early:
        operands = [early[own], *project(early, own, weights, gate_bias), *operands]
    return pl.pallas_call(
        functools.partial(attend_kernel, bool(early), own, items, *packing),
        out_shape=jax.ShapeDtypeStruct(late[0].shape, jnp.bfloat16),
        in_specs=[vmem] * len(operands),
        out_specs=vmem,
        scratch_shapes=[pltpu.VMEM(late[0].shape, jnp.float32)],
        compiler_params=pltpu.CompilerParams(
            vmem_limit_bytes=sum(v.size * v.dtype.itemsize for v in operands) + 16 * 2**20
        ),
    )(*operands)


def shifts(size):
    return sorted(range(1, size), key=lambda s: (min(s, size - s), s))


def send(values, to):
    orig_size, dest_size = lax.axis_size("orig"), lax.axis_size("dest")
    pairs = []
    for o in range(orig_size):
        for d in range(dest_size):
            far_o, far_d = to(o, d)
            pairs.append((o * dest_size + d, far_o * dest_size + far_d))
    return lax.ppermute(values, ("orig", "dest"), pairs)


def body(
    pair_field,
    region_mask,
    region_count,
    row_query,
    row_key,
    row_value,
    row_gate,
    row_gate_bias,
    row_out,
    col_query,
    col_key,
    col_value,
    col_gate,
    col_gate_bias,
    col_out,
):
    tile_rows, tile_cols, channels = pair_field.shape
    dest_size = lax.axis_size("dest")
    orig_size = lax.axis_size("orig")
    regions = region_mask.shape[0]
    row_steps = shifts(dest_size) + [0]
    chip_steps = shifts(orig_size // 2)

    def along_dest(d, step):
        return reverse((reverse(d, dest_size) + step) % dest_size, dest_size)

    def along_orig(o, step, flip):
        return (o // 2 + step) % (orig_size // 2) * 2 + (o % 2 ^ flip)

    row_sources = [lambda d, s=s: along_dest(d, dest_size - s) for s in row_steps]
    col_sources = [lambda o: o, lambda o: o ^ 1]
    for flip in (0, 1):
        col_sources += [
            lambda o, s=s, flip=flip: along_orig(o, orig_size // 2 - s, flip) for s in chip_steps
        ]
    row_packing = packing(tile_rows, regions)
    col_packing = packing(tile_cols, regions)
    rows = tile_rows * tile_cols
    prepared = prepare(
        ("dest", "orig"),
        (row_sources, col_sources),
        (tile_cols, tile_rows),
        (row_packing[0], col_packing[0]),
        region_mask,
        region_count,
        (row_query, row_gate, row_key, row_value, row_out)
        + (col_query, col_gate, col_key, col_value, col_out),
        (row_gate_bias, col_gate_bias),
    )

    tile = pair_field.reshape(rows, channels)
    blocks = [send(tile, lambda o, d: (o ^ 1, along_dest(d, s))) for s in row_steps]
    turned = attend([], blocks, row_steps.index(0), tile_rows, row_packing, prepared[:3])
    own = send(turned, lambda o, d: (o ^ 1, d))
    near = [send(turned, lambda o, d: (along_orig(o, s, 1), d)) for s in chip_steps]
    other = [send(block, lambda o, d: (o ^ 1, d)) for block in near]
    blocks = [own, turned, *near, *other]
    early = len(blocks) - 1 if (len(blocks) - 1) * rows <= group_rows else 0
    result = attend(blocks[:early], blocks[early:], 0, tile_cols, col_packing, prepared[3:])
    return result.reshape(tile_rows, tile_cols, channels)


def solution(mesh):
    tile = P("orig", "dest", None)
    in_specs = (tile,) + (P(),) * 14
    return jax.shard_map(body, mesh=mesh, in_specs=in_specs, out_specs=tile, check_vma=False)
```

```python
import functools
import math

import jax
import jax.numpy as jnp
from jax import lax
from jax.experimental import pallas as pl
from jax.experimental.pallas import tpu as pltpu
from jax.sharding import PartitionSpec as P

H = 4

epsilon = 1e-05
masked_score = -1e30
lanes = 128
group_rows = 1024

vmem = pl.BlockSpec(memory_space=pltpu.VMEM)


def packing(items, length):
    pack = max(p for p in range(1, items + 1) if items % p == 0 and (p == 1 or p * length <= lanes))
    group = max(
        g
        for g in range(pack, items + 1, pack)
        if items % g == 0 and (g == pack or g * length <= group_rows)
    )
    return pack, group


def gray(index):
    return index ^ (index >> 1)


def gray_place(index, size):
    place = index
    for shift in range(1, size.bit_length() - 1):
        place = place ^ (index >> shift)
    return place


def prepare_kernel(sources, parts, packs, mask_ref, count_ref, *refs):
    weights, gate_biases, outs = refs[:10], refs[10:12], refs[12:18]
    held_mask_ref, sem = refs[18:]
    channels = weights[0].shape[1]
    copies = [pltpu.make_async_copy(mask_ref, held_mask_ref, sem.at[0])]
    for a in range(2):
        for w in range(5):
            copies.append(
                pltpu.make_async_copy(
                    weights[5 * a + w].at[0],
                    outs[3 * a].at[:, pl.ds(w * channels, channels)],
                    sem.at[len(copies)],
                )
            )
        copies.append(pltpu.make_async_copy(gate_biases[a], outs[3 * a + 1], sem.at[len(copies)]))
    for copy in copies:
        copy.start()
    copies.pop(0).wait()
    regions = mask_ref.shape[1]
    place = lax.broadcasted_iota(jnp.int32, (8, regions), 1)
    valid = ((held_mask_ref[...] == 1) | (place == 0)) & (place < count_ref[0])
    valid = jnp.where(valid, 1.0, 0.0).astype(jnp.bfloat16)
    me = lax.axis_index("orig"), lax.axis_index("dest")
    for a in range(2):
        part, pack = parts[a], packs[a]
        shape = (regions, pack * regions)
        lane = lax.broadcasted_iota(jnp.int32, (1, shape[1]), 1)
        block = lane // (part * pack)
        region = lane % part
        for b, source in enumerate(sources[a]):
            region += jnp.where(block == b, source(*me) * part, 0)
        hit = lax.broadcasted_iota(jnp.int32, shape, 0) == region
        found = jnp.dot(
            valid, jnp.where(hit, 1.0, 0.0).astype(jnp.bfloat16), preferred_element_type=jnp.float32
        )
        outs[3 * a + 2][...] = jnp.where(found[:1] > 0.5, 0.0, masked_score)
    for copy in copies:
        copy.wait()


def prepare(sources, parts, packs, region_mask, region_count, weights, gate_biases):
    regions = region_mask.shape[0]
    channels = weights[0].shape[-1]
    outs = []
    for pack in packs:
        outs += [
            pltpu.VMEM((channels, 5 * channels), jnp.bfloat16),
            pltpu.VMEM((1, channels), jnp.float32),
            pltpu.VMEM((1, pack * regions), jnp.float32),
        ]
    return pl.pallas_call(
        functools.partial(prepare_kernel, sources, parts, packs),
        out_shape=tuple(outs),
        in_specs=[pl.BlockSpec(memory_space=pltpu.HBM), pl.BlockSpec(memory_space=pltpu.SMEM)]
        + [pl.BlockSpec(memory_space=pltpu.HBM)] * 12,
        out_specs=(vmem,) * 6,
        scratch_shapes=[pltpu.VMEM((1, regions), jnp.int32), pltpu.SemaphoreType.DMA((13,))],
        compiler_params=pltpu.CompilerParams(vmem_limit_bytes=16 * 2**20),
        cost_estimate=pl.CostEstimate(flops=2**20, bytes_accessed=2**20, transcendentals=0),
    )(
        pltpu.with_memory_space_constraint(region_mask.reshape(1, regions), pltpu.HBM),
        region_count,
        *(pltpu.with_memory_space_constraint(w, pltpu.HBM) for w in (*weights, *gate_biases)),
    )


def normalize(x):
    channels = x.shape[1]
    averaging = jnp.full((channels, channels), 1.0 / channels, jnp.bfloat16)
    mean = jnp.dot(x, averaging, preferred_element_type=jnp.float32)
    centered = x.astype(jnp.float32) - mean
    variance = jnp.mean(centered * centered, axis=1, keepdims=True)
    return (centered * lax.rsqrt(variance + epsilon)).astype(jnp.bfloat16)


def keys_and_values(normed, weight_ref):
    channels = weight_ref.shape[0]
    return tuple(
        jnp.dot(
            normed, weight_ref[:, w * channels : (w + 1) * channels], preferred_element_type=jnp.float32
        ).astype(jnp.bfloat16)
        for w in (2, 3)
    )


def queries_and_gate(normed, weight_ref, gate_bias_ref):
    channels = weight_ref.shape[0]
    products = jnp.dot(normed, weight_ref[:, : 2 * channels], preferred_element_type=jnp.float32)
    return products[:, :channels], jax.nn.sigmoid(products[:, channels:] + gate_bias_ref[...])


def project_kernel(own, *refs):
    *block_refs, weight_ref, gate_bias_ref, query_ref, gate_ref, key_ref, value_ref = refs
    rows = query_ref.shape[0]
    normed = normalize(jnp.concatenate([ref[...] for ref in block_refs], 0))
    queries, gate_ref[...] = queries_and_gate(
        normed[own * rows : (own + 1) * rows], weight_ref, gate_bias_ref
    )
    query_ref[...] = queries.astype(jnp.bfloat16)
    key_ref[...], value_ref[...] = keys_and_values(normed, weight_ref)


def attend_kernel(split, own, items, pack, group, *refs):
    weight_ref, gate_bias_ref, bias_ref, out_ref, turned_ref = refs[-5:]
    rows, channels = out_ref.shape
    if split:
        own_ref, query_ref, gate_ref, key_ref, value_ref, *late_refs = refs[:-5]
    else:
        late_refs = refs[:-5]
        own_ref = late_refs[own]
    early = key_ref.shape[0] // rows if split else 0
    head_size = channels // H
    part = rows // items
    step_rows, pack_rows = group * part, pack * part
    blocks = early + len(late_refs)
    scale = math.log2(math.e) / math.sqrt(head_size)
    head_of = lax.broadcasted_iota(jnp.int32, (1, channels), 1) // head_size
    shape = (H * pack_rows, blocks * pack_rows)
    row_item = lax.broadcasted_iota(jnp.int32, shape, 0) // part % pack
    key_item = lax.broadcasted_iota(jnp.int32, shape, 1) // part % pack
    bias = jnp.where(row_item == key_item, bias_ref[...], masked_score)

    def step(start):
        here = pl.ds(start, step_rows)
        normed = normalize(jnp.concatenate([ref[here] for ref in late_refs], 0))
        if split:
            queries, gate = query_ref[here].astype(jnp.float32), gate_ref[here]
        else:
            queries, gate = queries_and_gate(
                normed[own * step_rows : (own + 1) * step_rows], weight_ref, gate_bias_ref
            )
        late_keys, late_values = keys_and_values(normed, weight_ref)
        packs = range(group // pack)

        def by_pack(early_ref, late):
            products = [early_ref[pl.ds(b * rows + start, step_rows)] for b in range(early)]
            products += [
                late[b * step_rows : (b + 1) * step_rows] for b in range(len(late_refs))
            ]
            return [
                jnp.concatenate([p[i * pack_rows : (i + 1) * pack_rows] for p in products], 0)
                for i in packs
            ]

        keys = by_pack(key_ref if split else None, late_keys)
        values = by_pack(value_ref if split else None, late_values)
        scores = []
        for i in packs:
            query = queries[i * pack_rows : (i + 1) * pack_rows]
            stacked = jnp.concatenate([jnp.where(head_of == h, query, 0.0) for h in range(H)], 0)
            scores.append(
                lax.dot_general(
                    stacked.astype(jnp.bfloat16),
                    keys[i],
                    (((1,), (1,)), ((), ())),
                    preferred_element_type=jnp.float32,
                )
                * scale
                + bias
            )
        scores = jnp.concatenate(scores, 0)
        expanded = jnp.exp2(scores - jnp.max(scores, axis=1, keepdims=True))
        weights = (expanded * (1.0 / jnp.sum(expanded, axis=1, keepdims=True))).astype(jnp.bfloat16)
        attended = []
        for i in packs:
            at = slice(i * H * pack_rows, (i + 1) * H * pack_rows)
            heads = jnp.dot(weights[at], values[i], preferred_element_type=jnp.float32)
            picked = heads[:pack_rows]
            for h in range(1, H):
                picked = jnp.where(
                    head_of == h, heads[h * pack_rows : (h + 1) * pack_rows], picked
                )
            attended.append(picked)
        attended = jnp.concatenate(attended, 0).astype(jnp.bfloat16).astype(jnp.float32)
        gated = (gate * attended).astype(jnp.bfloat16)
        return own_ref[here].astype(jnp.float32) + jnp.dot(
            gated, weight_ref[:, 4 * channels :], preferred_element_type=jnp.float32
        )

    def one_group(g, start):
        result = step(start)
        for i in range(group):
            turned_ref[pl.ds(g * group + i, part, stride=items), :] = result[
                i * part : (i + 1) * part
            ]

    if group == items:
        one_group(0, 0)
    else:

        def body(g, carry):
            one_group(g, pl.multiple_of(g * step_rows, step_rows))
            return carry

        lax.fori_loop(0, items // group, body, 0)
    out_ref[...] = turned_ref[...].astype(out_ref.dtype)


def project(blocks, own, weights, gate_bias):
    rows, channels = blocks[0].shape
    return pl.pallas_call(
        functools.partial(project_kernel, own),
        out_shape=(
            jax.ShapeDtypeStruct((rows, channels), jnp.bfloat16),
            jax.ShapeDtypeStruct((rows, channels), jnp.float32),
            jax.ShapeDtypeStruct((len(blocks) * rows, channels), jnp.bfloat16),
            jax.ShapeDtypeStruct((len(blocks) * rows, channels), jnp.bfloat16),
        ),
        in_specs=[vmem] * (len(blocks) + 2),
        out_specs=(vmem,) * 4,
        compiler_params=pltpu.CompilerParams(
            vmem_limit_bytes=8 * len(blocks) * rows * channels + 16 * 2**20
        ),
    )(*blocks, weights, gate_bias)


def attend(early, late, own, items, packing, prepared):
    weights, gate_bias, bias = prepared
    operands = [*late, *prepared]
    if early:
        operands = [early[own], *project(early, own, weights, gate_bias), *operands]
    return pl.pallas_call(
        functools.partial(attend_kernel, bool(early), own, items, *packing),
        out_shape=jax.ShapeDtypeStruct(late[0].shape, jnp.bfloat16),
        in_specs=[vmem] * len(operands),
        out_specs=vmem,
        scratch_shapes=[pltpu.VMEM(late[0].shape, jnp.float32)],
        compiler_params=pltpu.CompilerParams(
            vmem_limit_bytes=sum(v.size * v.dtype.itemsize for v in operands) + 16 * 2**20
        ),
    )(*operands)


def shifts(size):
    return sorted(range(1, size), key=lambda s: (min(s, size - s), s))


def send(values, to):
    orig_size, dest_size = lax.axis_size("orig"), lax.axis_size("dest")
    pairs = []
    for o in range(orig_size):
        for d in range(dest_size):
            far_o, far_d = to(o, d)
            pairs.append((o * dest_size + d, far_o * dest_size + far_d))
    return lax.ppermute(values, ("orig", "dest"), pairs)


def body(
    pair_field,
    region_mask,
    region_count,
    row_query,
    row_key,
    row_value,
    row_gate,
    row_gate_bias,
    row_out,
    col_query,
    col_key,
    col_value,
    col_gate,
    col_gate_bias,
    col_out,
):
    tile_rows, tile_cols, channels = pair_field.shape
    dest_size = lax.axis_size("dest")
    orig_size = lax.axis_size("orig")
    regions = region_mask.shape[0]
    row_steps = [*range(1, dest_size), 0]
    chip_steps = shifts(orig_size // 2)

    def along_dest(d, step, odd):
        plain = (d + step) % dest_size
        return plain + odd * (gray((gray_place(d, dest_size) + step) % dest_size) - plain)

    def along_orig(o, step, flip):
        return (o // 2 + step) % (orig_size // 2) * 2 + (o % 2 ^ flip)

    row_sources = [
        lambda o, d, s=s: along_dest(d, dest_size - s, 1 - o % 2) for s in row_steps
    ]
    col_sources = [lambda o, d: o, lambda o, d: o ^ 1]
    for flip in (0, 1):
        col_sources += [
            lambda o, d, s=s, flip=flip: along_orig(o, orig_size // 2 - s, flip) for s in chip_steps
        ]
    row_packing = packing(tile_rows, regions)
    col_packing = packing(tile_cols, regions)
    rows = tile_rows * tile_cols
    prepared = prepare(
        (row_sources, col_sources),
        (tile_cols, tile_rows),
        (row_packing[0], col_packing[0]),
        region_mask,
        region_count,
        (row_query, row_gate, row_key, row_value, row_out)
        + (col_query, col_gate, col_key, col_value, col_out),
        (row_gate_bias, col_gate_bias),
    )

    tile = pair_field.reshape(rows, channels)
    blocks = [send(tile, lambda o, d: (o ^ 1, along_dest(d, s, o % 2))) for s in row_steps]
    turned = attend([], blocks, row_steps.index(0), tile_rows, row_packing, prepared[:3])
    own = send(turned, lambda o, d: (o ^ 1, d))
    near = [send(turned, lambda o, d: (along_orig(o, s, 1), d)) for s in chip_steps]
    other = [send(block, lambda o, d: (o ^ 1, d)) for block in near]
    blocks = [own, turned, *near, *other]
    early = len(blocks) - 1 if (len(blocks) - 1) * rows <= group_rows else 0
    result = attend(blocks[:early], blocks[early:], 0, tile_cols, col_packing, prepared[3:])
    return result.reshape(tile_rows, tile_cols, channels)


def solution(mesh):
    tile = P("orig", "dest", None)
    in_specs = (tile,) + (P(),) * 14
    return jax.shard_map(body, mesh=mesh, in_specs=in_specs, out_specs=tile, check_vma=False)
```
